128 devices in a mesh: lat: 4 (over z_hi, core), lon: 32 (over x, y, z_lo).
Axes of the slice: x: 4, y: 4, z: 4 (z_hi: 2, z_lo: 2; z = z_hi * 2 + z_lo), core: 2. Of those that a mesh axis runs over, the one named last changes fastest.
Arguments:
- coarse: bfloat16 [384, 1024, 384], P('lat', 'lon'), may hold values from -6 to 6
- ocean_tiles: int32 [12, 32], P('lat', 'lon'), may hold values from 0 to 1, as said below
- dw_weight: float32 [2, 7, 7, 384], replicated, may hold values from -0.875 to 0.875
- dw_bias: float32 [2, 384], replicated, may hold values from -3 to 3
- norm_gain: float32 [2, 384], replicated, may hold values from 0.5 to 1.5
- norm_shift: float32 [2, 384], replicated, may hold values from -3 to 3
- in_weight: bfloat16 [2, 384, 768], replicated, may hold values from -0.3125 to 0.3125
- in_bias: float32 [2, 768], replicated, may hold values from -3 to 3
- out_weight: bfloat16 [2, 768, 384], replicated, may hold values from -0.21875 to 0.21875
- out_bias: float32 [2, 384], replicated, may hold values from -3 to 3
- layer_scale: float32 [2, 384], replicated, may hold values from 0.3 to 1
- up_weight: bfloat16 [3, 3, 384, 192], replicated, may hold values from -0.15625 to 0.15625
- up_bias: float32 [192], replicated, may hold values from -3 to 3
Outputs:
- fine: bfloat16 [768, 2048, 192], P(('lat', 'lon'))
The draws below stay inside these ranges and needn't reach their ends.
Inputs may be any that keep to these rules, and one draw needn't show every extreme that they name: `ocean_tiles`: 1 marks a tile with ocean, 0 an all-land tile. The tiles are partitioned evenly: each aligned block of 3 by 1 tiles (those of one device) holds exactly max(1, K // 3) land tiles, with K the tiles of the block.
All inputs are finite; a program needn't handle non-finite values.
Results may differ from the reference program's by a relative error of at most 0.0075.
Values may be sent and summed in bfloat16 or wider, within the bound.
A program may use at most 128 MiB of HBM per device.

```python
import jax
import jax.numpy as jnp
from jax import lax

C = 384
HID = 768
CO = 192
LAYERS = 2
TS = 32
CLAT = 96
CLON = 32
HEIGHT = 384
WIDTH = 1024
TILE_ROWS = 12
TILE_COLS = 32


def draw_ocean_tiles(key, part):
    block_tile_rows = CLAT // TS
    block_tile_cols = CLON // TS
    per_block = block_tile_rows * block_tile_cols
    band_count = TILE_ROWS // block_tile_rows
    column_count = TILE_COLS // block_tile_cols
    land_count = max(1, per_block // 3)
    block_keys = jax.random.split(key, band_count * column_count)
    orders = jax.vmap(lambda single: jax.random.permutation(single, per_block))(block_keys)
    ocean = (orders >= land_count).astype(jnp.int32)
    ocean = ocean.reshape(band_count, column_count, block_tile_rows, block_tile_cols)
    return ocean.transpose(0, 2, 1, 3).reshape(TILE_ROWS, TILE_COLS)


def shard_levels(rng, extent, cuts, smallest, largest):
    factor_of, own = 1.0, jax.random.fold_in(rng, 6)
    for dim, shards_of in cuts:
        heights = jnp.exp(jax.random.uniform(jax.random.fold_in(own, dim), (shards_of,), jnp.float32, smallest / len(cuts), largest / len(cuts)))
        factor_of = factor_of * jnp.repeat(heights, extent[dim] // shards_of).reshape([-1 if axis == dim else 1 for axis in range(len(extent))])
    return factor_of


def bell_draw(key, dims, scale, most, cuts=(), kind=jnp.bfloat16):
    entries = scale * jax.random.normal(key, dims, jnp.float32)
    if cuts:
        entries = entries * shard_levels(key, dims, cuts, -0.22, 0.18)
    return jnp.clip(entries, -most, most).astype(kind)


def setup_inputs(seed: int = 0) -> dict:
    splits = jax.random.split(jax.random.key(seed), 14)
    coarse = bell_draw(splits[0], (HEIGHT, WIDTH, C), 1.0, 6.0, ((0, 4), (1, 32)))
    ocean_tiles = draw_ocean_tiles(jax.random.fold_in(splits[13], 71), 0)
    dw_weight = bell_draw(splits[2], (LAYERS, 7, 7, C), 49 ** -0.5, 0.875, (), jnp.float32)
    dw_bias = bell_draw(splits[3], (LAYERS, C), 0.5, 3.0, (), jnp.float32)
    norm_gain = jnp.clip(1.0 + 0.1 * jax.random.normal(splits[4], (LAYERS, C), jnp.float32), 0.5, 1.5)
    norm_shift = bell_draw(splits[5], (LAYERS, C), 0.3, 3.0, (), jnp.float32)
    in_weight = bell_draw(splits[6], (LAYERS, C, HID), C ** -0.5, 0.3125)
    in_bias = bell_draw(splits[7], (LAYERS, HID), 0.5, 3.0, (), jnp.float32)
    out_weight = bell_draw(splits[8], (LAYERS, HID, C), HID ** -0.5, 0.21875)
    out_bias = bell_draw(splits[9], (LAYERS, C), 0.3, 3.0, (), jnp.float32)
    layer_scale = jnp.clip(jax.random.uniform(splits[10], (LAYERS, C), jnp.float32, 0.3, 1.0), 0.3, 1.0)
    up_weight = bell_draw(splits[11], (3, 3, C, CO), (4 * C) ** -0.5, 0.15625)
    up_bias = bell_draw(splits[12], (CO,), 0.3, 3.0, (), jnp.float32)
    return dict(coarse=coarse, ocean_tiles=ocean_tiles, dw_weight=dw_weight, dw_bias=dw_bias, norm_gain=norm_gain, norm_shift=norm_shift, in_weight=in_weight, in_bias=in_bias, out_weight=out_weight, out_bias=out_bias, layer_scale=layer_scale, up_weight=up_weight, up_bias=up_bias)


block_rows = 8

def depthwise(padded, weights, bias, row_count, column_count):
    total = jnp.zeros((row_count, column_count, padded.shape[2]), jnp.float32)
    for row_tap in range(7):
        for column_tap in range(7):
            window = padded[row_tap:row_tap + row_count, column_tap:column_tap + column_count]
            total = total + window.astype(jnp.float32) * weights[row_tap, column_tap]
    return total + bias

def mixer(depth, gain, shift, in_weight, in_bias, out_weight, out_bias):
    channels = depth.shape[-1]
    center = lax.optimization_barrier(jnp.mean(depth, -1, keepdims=True))
    offset = depth - center
    spread = lax.optimization_barrier(jnp.mean(offset * offset, -1, keepdims=True))
    normed = (offset * lax.rsqrt(spread + 1e-06) * gain + shift).astype(jnp.bfloat16)
    flat = normed.reshape(-1, channels)
    hidden = jax.nn.gelu(jnp.dot(flat, in_weight, preferred_element_type=jnp.float32) + in_bias, approximate=True).astype(jnp.bfloat16)
    result = jnp.dot(hidden, out_weight, preferred_element_type=jnp.float32) + out_bias
    return result.reshape(depth.shape)

def upsample(extended, weight, bias):
    row_count = extended.shape[0] - 1
    column_count = extended.shape[1] - 1
    channels = extended.shape[2]
    width_out = weight.shape[3]
    current_cell = extended[:-1, :-1].reshape(-1, channels)
    right_cell = extended[:-1, 1:].reshape(-1, channels)
    lower_cell = extended[1:, :-1].reshape(-1, channels)
    corner_cell = extended[1:, 1:].reshape(-1, channels)
    direct = jnp.dot(current_cell, jnp.concatenate([weight[1, 1], weight[1, 2], weight[2, 1], weight[2, 2]], 1), preferred_element_type=jnp.float32)
    beside = jnp.dot(right_cell, jnp.concatenate([weight[1, 0], weight[2, 0]], 1), preferred_element_type=jnp.float32)
    beneath = jnp.dot(lower_cell, jnp.concatenate([weight[0, 1], weight[0, 2]], 1), preferred_element_type=jnp.float32)
    diagonal_term = jnp.dot(corner_cell, weight[0, 0], preferred_element_type=jnp.float32)
    phase_even_even = direct[:, :width_out]
    phase_even_odd = direct[:, width_out:2 * width_out] + beside[:, :width_out]
    phase_odd_even = direct[:, 2 * width_out:3 * width_out] + beneath[:, :width_out]
    phase_odd_odd = direct[:, 3 * width_out:] + beside[:, width_out:] + beneath[:, width_out:] + diagonal_term
    upper_rows = jnp.stack([phase_even_even, phase_even_odd], 1).reshape(row_count, 2 * column_count, width_out)
    bottom_rows = jnp.stack([phase_odd_even, phase_odd_odd], 1).reshape(row_count, 2 * column_count, width_out)
    whole = jnp.stack([upper_rows, bottom_rows], 1).reshape(2 * row_count, 2 * column_count, width_out)
    return (whole + bias).astype(jnp.bfloat16)

def reference(coarse, ocean_tiles, dw_weight, dw_bias, norm_gain, norm_shift, in_weight, in_bias, out_weight, out_bias, layer_scale, up_weight, up_bias):
    height = coarse.shape[0]
    width = coarse.shape[1]
    cell_mask = jnp.repeat(jnp.repeat(ocean_tiles, TS, 0), TS, 1).astype(jnp.float32)
    starts = jnp.arange(height // block_rows, dtype=jnp.int32) * block_rows
    field = coarse
    for layer_index in range(LAYERS):
        padded = jnp.concatenate([field[:, -3:], field, field[:, :3]], 1)
        padded = jnp.pad(padded, ((3, 3), (0, 0), (0, 0)))

        def block_update(start, padded=padded, field=field, layer_index=layer_index):
            slab = lax.dynamic_slice_in_dim(padded, start, block_rows + 6, 0)
            depth = depthwise(slab, dw_weight[layer_index], dw_bias[layer_index], block_rows, width)
            update = mixer(depth, norm_gain[layer_index], norm_shift[layer_index], in_weight[layer_index], in_bias[layer_index], out_weight[layer_index], out_bias[layer_index])
            base = lax.dynamic_slice_in_dim(field, start, block_rows, 0)
            masked = lax.dynamic_slice_in_dim(cell_mask, start, block_rows, 0)
            return (base.astype(jnp.float32) + masked[..., None] * layer_scale[layer_index] * update).astype(jnp.bfloat16)
        field = lax.map(block_update, starts).reshape(height, width, -1)
    extended = jnp.concatenate([field, field[:, :1]], 1)
    extended = jnp.pad(extended, ((0, 1), (0, 0), (0, 0)))

    def fine_block(start):
        slab = lax.dynamic_slice_in_dim(extended, start, block_rows + 1, 0)
        return upsample(slab, up_weight, up_bias)
    result = lax.map(fine_block, starts)
    return result.reshape(2 * height, 2 * width, -1)
```

```python
import functools
import jax
import jax.numpy as jnp
from jax import lax
from jax.experimental import pallas as pl
from jax.experimental.pallas import tpu as pltpu

TS = 32
R = 8
COL0 = 8


def depthwise_block(x_ref, wb_ref, bias, d_ref, row0, groups):
    for g in range(groups):
        for cb in range(4):
            total = jnp.zeros((R, 8, 128), jnp.float32)
            for b in range(7):
                start = COL0 - 3 + b + 8 * cb
                window = x_ref[g, pl.ds(row0, R + 6), start : start + 8, :]
                for a in range(7):
                    total = total + window[a : a + R] * wb_ref[a * 7 + b, g]
            d_ref[:, 8 * cb : 8 * cb + 8, 128 * g : 128 * g + 128] = (
                total + bias[:, 128 * g : 128 * g + 128]
            )


def mix_block(depth, gain, shift, w_in, b_in, w_out, b_out):
    center = jnp.mean(depth, -1, keepdims=True)
    offset = depth - center
    spread = jnp.mean(offset * offset, -1, keepdims=True)
    normed = (offset * lax.rsqrt(spread + 1e-06) * gain + shift).astype(jnp.bfloat16)
    hidden = jnp.dot(normed, w_in, preferred_element_type=jnp.float32) + b_in
    inner = hidden * (0.7978845608028654 + 0.035677408136300125 * (hidden * hidden))
    half = 0.5 * hidden
    hidden = (half + half * jnp.tanh(inner)).astype(jnp.bfloat16)
    return jnp.dot(hidden, w_out, preferred_element_type=jnp.float32) + b_out


def layer_kernel(tiles_ref, pad_ref, dw_ref, dwb_ref, gain_ref, shift_ref, win_ref, bin_ref,
                 wout_ref, bout_ref, scale_ref, out_ref, x_ref, wb_ref, d_ref):
    height, width, channels = out_ref.shape
    groups = channels // 128
    for k in range(49):
        for g in range(groups):
            wb_ref[k, g] = jnp.broadcast_to(dw_ref[k : k + 1, 128 * g : 128 * g + 128], (8, 128))

    @pl.loop(0, (height + 6) // 6)
    def _(i):
        rows = pl.ds(i * 6, 6)
        for g in range(groups):
            x_ref[g, rows] = pad_ref[rows, :, 128 * g : 128 * g + 128].astype(jnp.float32)

    blocks = TS // R
    m0, m1, m2 = tiles_ref[0, 0], tiles_ref[1, 0], tiles_ref[2, 0]
    for t in range(3):
        @pl.when(tiles_ref[t, 0] == 0)
        def _():
            out_ref[TS * t : TS * t + TS] = pad_ref[3 + TS * t : 3 + TS * t + TS, COL0 : COL0 + width]

        @pl.when(tiles_ref[t, 0] != 0)
        def _():
            @pl.loop(0, blocks)
            def _(i):
                row0 = t * TS + i * R
                depthwise_block(x_ref, wb_ref, dwb_ref[...], d_ref, row0, groups)
                update = mix_block(d_ref[...].reshape(R * width, channels), gain_ref[...], shift_ref[...],
                                   win_ref[...], bin_ref[...], wout_ref[...], bout_ref[...])
                field = pad_ref[pl.ds(3 + row0, R), COL0 : COL0 + width].astype(jnp.float32)
                mask = tiles_ref[t, 0].astype(jnp.float32)
                out_ref[pl.ds(row0, R)] = (
                    field + (mask * scale_ref[...]) * update.reshape(R, width, channels)
                ).astype(jnp.bfloat16)


def layer_call(tiles, padded, *params):
    height, width, channels = padded.shape[0] - 6, padded.shape[1] - 16, padded.shape[2]
    vmem = pl.BlockSpec(memory_space=pltpu.VMEM)
    return pl.pallas_call(
        layer_kernel,
        out_shape=jax.ShapeDtypeStruct((height, width, channels), jnp.bfloat16),
        in_specs=[pl.BlockSpec(memory_space=pltpu.SMEM)] + [vmem] * (1 + len(params)),
        out_specs=vmem,
        scratch_shapes=[
            pltpu.VMEM((channels // 128, height + 6, width + 16, 128), jnp.float32),
            pltpu.VMEM((49, channels // 128, 8, 128), jnp.float32),
            pltpu.VMEM((R, width, channels), jnp.float32),
        ],
        compiler_params=pltpu.CompilerParams(vmem_limit_bytes=48 * 1024 * 1024),
    )(tiles, padded, *params)


UCH = 256


def upsample_kernel(y_ref, next_ref, w_ee, w_eo, w_oe, w_oo, bias_ref, out_ref, f_ref):
    width_out = out_ref.shape[2]
    wides = []
    for i in range(4):
        cur = y_ref[i]
        both = jnp.concatenate([cur, next_ref[i]], 0).astype(jnp.float32)
        right = both[1 : 1 + UCH].astype(jnp.bfloat16)
        wides.append((cur, right))
    bias = bias_ref[...]
    for i in range(3):
        cur, right = wides[i]
        low, corner = wides[i + 1]
        ee = jnp.dot(cur, w_ee[...], preferred_element_type=jnp.float32) + bias
        eo = jnp.dot(jnp.concatenate([cur, right], 1), w_eo[...], preferred_element_type=jnp.float32) + bias
        oe = jnp.dot(jnp.concatenate([cur, low], 1), w_oe[...], preferred_element_type=jnp.float32) + bias
        oo = jnp.dot(jnp.concatenate([cur, right, low, corner], 1), w_oo[...], preferred_element_type=jnp.float32) + bias
        for p, (even, odd) in enumerate(((ee, eo), (oe, oo))):
            for k, lanes in enumerate((slice(0, 128), slice(128, width_out))):
                wide = lanes.stop - lanes.start
                f_ref[k, pl.ds(0, UCH, stride=2), :wide] = even[:, lanes]
                f_ref[k, pl.ds(1, UCH, stride=2), :wide] = odd[:, lanes]
                out_ref[2 * i + p, :, lanes] = f_ref[k, :, :wide].astype(jnp.bfloat16)


def upsample_call(y, weight, bias):
    rows, width, channels = y.shape
    out_width = weight.shape[3]
    w_ee = weight[1, 1]
    w_eo = jnp.concatenate([weight[1, 2], weight[1, 0]], 0)
    w_oe = jnp.concatenate([weight[2, 1], weight[0, 1]], 0)
    w_oo = jnp.concatenate([weight[2, 2], weight[2, 0], weight[0, 2], weight[0, 0]], 0)
    chunks = width // UCH
    whole = lambda w: pl.BlockSpec(w.shape, lambda j: (0,) * w.ndim)
    bias = bias.reshape(1, -1)
    return pl.pallas_call(
        upsample_kernel,
        grid=(chunks,),
        out_shape=jax.ShapeDtypeStruct((2 * rows - 2, 2 * width, out_width), jnp.bfloat16),
        in_specs=[
            pl.BlockSpec((rows, UCH, channels), lambda j: (0, j, 0)),
            pl.BlockSpec((rows, 16, channels), lambda j: (0, ((j + 1) % chunks) * (UCH // 16), 0)),
            whole(w_ee), whole(w_eo), whole(w_oe), whole(w_oo), whole(bias),
        ],
        out_specs=pl.BlockSpec((2 * rows - 2, 2 * UCH, out_width), lambda j: (0, j, 0)),
        scratch_shapes=[pltpu.VMEM((2, 2 * UCH, 128), jnp.float32)],
        compiler_params=pltpu.CompilerParams(vmem_limit_bytes=48 * 1024 * 1024),
    )(y, y, w_ee, w_eo, w_oe, w_oo, bias)


def local(coarse, ocean_tiles, dw_weight, dw_bias, norm_gain, norm_shift, in_weight, in_bias,
          out_weight, out_bias, layer_scale, up_weight, up_bias):
    height, width, channels = coarse.shape
    size = lax.axis_size("lon")
    up = [(i, (i + 1) % size) for i in range(size)]
    down = [(j, i) for i, j in up]
    lat_up = [(i, i + 1) for i in range(lax.axis_size("lat") - 1)]
    lat_down = [(j, i) for i, j in lat_up]
    field = coarse
    for l in range(2):
        before = lax.ppermute(field[:, -3:], "lon", up)
        after = lax.ppermute(field[:, :3], "lon", down)
        wide = jnp.concatenate([before, field, after], 1)
        above = lax.ppermute(wide[-3:], "lat", lat_up)
        below = lax.ppermute(wide[:3], "lat", lat_down)
        padded = jnp.pad(jnp.concatenate([above, wide, below], 0), ((0, 0), (5, 5), (0, 0)))
        row = lambda v: v[l].reshape(1, -1)
        field = layer_call(ocean_tiles, padded, dw_weight[l].reshape(49, channels), row(dw_bias),
                           row(norm_gain), row(norm_shift), in_weight[l], row(in_bias),
                           out_weight[l], row(out_bias), row(layer_scale))
    below = lax.ppermute(field[:1], "lat", lat_down)
    owned = field.reshape(size, height // size, width, channels)
    last = jnp.concatenate([owned[1:, :1], below[None]], 0)
    sent = jnp.concatenate([owned, last], 1)
    got = lax.all_to_all(sent, "lon", split_axis=0, concat_axis=0, tiled=True)
    rows = got.transpose(1, 0, 2, 3).reshape(height // size + 1, size * width, channels)
    return upsample_call(rows, up_weight, up_bias)


def solution(mesh):
    from jax.sharding import PartitionSpec as P
    placed = (P("lat", "lon", None), P("lat", "lon")) + (P(),) * 11
    return jax.shard_map(
        local, mesh=mesh, in_specs=placed, out_specs=P(("lat", "lon"), None, None), check_vma=False
    )
```

```python
import jax
import jax.numpy as jnp
from jax import lax
from jax.experimental import pallas as pl
from jax.experimental.pallas import tpu as pltpu
from jax.sharding import PartitionSpec as P

TS = 32
COL0 = 8
MESH = pl.DeviceIdType.MESH
F32 = jnp.float32
BF16 = jnp.bfloat16


def depthwise_block(x_ref, wb_ref, bias_ref, d_ref, row0, rows, groups):
    for g in range(groups):
        for cb in range(4):
            total = jnp.zeros((rows, 8, 128), F32)
            for b in range(7):
                start = COL0 - 3 + b + 8 * cb
                window = x_ref[g, pl.ds(row0, rows + 6), start : start + 8, :]
                for a in range(7):
                    total = total + window[a : a + rows] * wb_ref[a * 7 + b, g]
            d_ref[g, :, 8 * cb : 8 * cb + 8, :] = total + bias_ref[g]


def mix_block(depth, gain, shift, w_in, b_in, w_out, b_out):
    center = jnp.mean(depth, -1, keepdims=True)
    offset = depth - center
    spread = jnp.mean(offset * offset, -1, keepdims=True)
    normed = (offset * lax.rsqrt(spread + 1e-06) * gain + shift).astype(BF16)
    hidden = jnp.dot(normed, w_in, preferred_element_type=F32) + b_in
    inner = hidden * (0.7978845608028654 + 0.035677408136300125 * (hidden * hidden))
    half = 0.5 * hidden
    hidden = (half + half * jnp.tanh(inner)).astype(BF16)
    return jnp.dot(hidden, w_out, preferred_element_type=F32) + b_out


def swap_halves(v):
    return jnp.concatenate([v[..., 4:, :], v[..., :4, :]], -2)


def first_half(shape):
    return lax.broadcasted_iota(jnp.int32, shape, len(shape) - 2) < 4


def pack_edges(low, high):
    rows, _, channels = low.shape
    low = low.reshape(rows // 2, 2, 8, channels)
    high = high.reshape(rows // 2, 2, 8, channels)
    pick = first_half((rows // 2, 8, channels))
    left = jnp.where(pick, low[:, 0], swap_halves(low[:, 1]))
    right = jnp.where(pick, swap_halves(high[:, 0]), high[:, 1])
    return [v.reshape(rows * 4, channels).astype(BF16) for v in (left, right)]


def section_kernel(tiles_ref, coarse_ref, dw_ref, dwb_ref, gain_ref, shift_ref, win_ref, bin_ref, wout_ref,
                   bout_ref, scale_ref, y_ref, x_ref, wb_ref, d_ref, u_ref, out_ref, edge_out, edge_in,
                   row_out, row_in, corner_in, halo_send, halo_recv, sems, group_sems):
    height, width, channels = coarse_ref.shape
    groups = channels // 128
    lat, lon = lax.axis_index("lat"), lax.axis_index("lon")
    nlat, nlon = lax.axis_size("lat"), lax.axis_size("lon")
    left, right = lax.rem(lon + nlon - 1, nlon), lax.rem(lon + 1, nlon)
    has_up, has_down = lat > 0, lat < nlat - 1
    owned = height // nlon
    rows = d_ref.shape[2]
    blocks = TS // rows

    barrier = pltpu.get_barrier_semaphore()

    def greet(a, b):
        pl.semaphore_signal(barrier, inc=1, device_id=(a, b), device_id_type=MESH)

    @pl.loop(1, nlon)
    def _(k):
        greet(lat, lax.rem(lon + k, nlon))

    for present, other in ((has_up, lat - 1), (has_down, lat + 1)):
        @pl.when(present)
        def _():
            for b in (left, lon, right):
                greet(other, b)

    @pl.when(jnp.logical_and(has_down, lon == nlon - 1))
    def _():
        @pl.loop(0, nlon)
        def _(k):
            greet(lat + 1, k)

    def edge_copies(l, row0, count):
        part = pl.ds(pl.multiple_of(row0 * 4, 16), count * 4)
        return [pltpu.make_async_remote_copy(
            src_ref=edge_out.at[l, k, part], dst_ref=edge_in.at[l, k, part],
            send_sem=halo_send.at[l, k], recv_sem=halo_recv.at[l, k],
            device_id=(lat, (left, right)[k]), device_id_type=MESH) for k in range(2)]

    def row_copies(l, k):
        other = lat - 1 if k == 0 else lat + 1
        part = pl.ds(0, 16) if k == 0 else pl.ds(height * 4 - 16, 16)
        copies = [pltpu.make_async_remote_copy(
            src_ref=row_out.at[l, k], dst_ref=row_in.at[l, k],
            send_sem=halo_send.at[l, 2 + k], recv_sem=halo_recv.at[l, 2 + k],
            device_id=(other, lon), device_id_type=MESH)]
        for e in range(2):
            copies.append(pltpu.make_async_remote_copy(
                src_ref=edge_out.at[l, e, part], dst_ref=corner_in.at[l, k, e],
                send_sem=halo_send.at[l, 4 + 2 * k + e], recv_sem=halo_recv.at[l, 4 + 2 * k + e],
                device_id=(other, (left, right)[e]), device_id_type=MESH))
        return copies

    m0, m1, m2 = tiles_ref[0, 0], tiles_ref[1, 0], tiles_ref[2, 0]
    first_tile = jnp.where(m0 != 0, 0, 1)
    second_tile = jnp.where(m2 != 0, 2, 1)
    masks = [m.astype(F32) for m in (m0, m1, m2)]

    @pl.loop(0, height // 8)
    def _(i):
        part = pl.ds(pl.multiple_of(i * 8, 8), 8)
        low = coarse_ref[part, 0:16, :].astype(F32)[:, 0:8]
        high = coarse_ref[part, width - 16 : width, :].astype(F32)[:, 8:16]
        packed = pack_edges(low, high)
        for k in range(2):
            edge_out[0, k, pl.ds(pl.multiple_of(i * 32, 32), 32)] = packed[k]

    row_out[0, 0] = coarse_ref[0:3]
    row_out[0, 1] = coarse_ref[height - 3 : height]

    pl.semaphore_wait(barrier, nlon - 1 + jnp.where(has_up, 4, 0) + jnp.where(has_down, 3, 0))
    for copy in edge_copies(0, 0, height):
        copy.start()
    for k, present in enumerate((has_up, has_down)):
        @pl.when(present)
        def _():
            for copy in row_copies(0, k):
                copy.start()

    @pl.loop(0, height // 8)
    def _(i):
        part = pl.ds(pl.multiple_of(i * 8, 8), 8)
        for g in range(groups):
            x_ref[0, g, pl.ds(i * 8 + 3, 8), COL0 : COL0 + width, :] = coarse_ref[
                part, :, 128 * g : 128 * g + 128].astype(F32)

    def chunk_copy(row, slot, a, b, which):
        return pltpu.make_async_remote_copy(
            src_ref=out_ref.at[row], dst_ref=y_ref.at[slot, pl.ds(pl.multiple_of(lon * width, 32), width)],
            send_sem=group_sems.at[0, which], recv_sem=group_sems.at[1, which],
            device_id=(a, b), device_id_type=MESH)

    def own_copy(row, slot):
        return pltpu.make_async_copy(
            out_ref.at[row], y_ref.at[slot, pl.ds(pl.multiple_of(lon * width, 32), width)], sems.at[slot])

    def send_row(row):
        owner = row // owned
        slot = row - owner * owned

        @pl.when(owner == lon)
        def _():
            own_copy(row, slot).start()

        @pl.when(owner != lon)
        def _():
            chunk_copy(row, slot, lat, owner, 0).start()

        @pl.when(slot == 0)
        def _():
            @pl.when(row == 0)
            def _():
                @pl.when(has_up)
                def _():
                    chunk_copy(row, owned, lat - 1, nlon - 1, 1).start()

            @pl.when(row > 0)
            def _():
                @pl.when(owner - 1 == lon)
                def _():
                    own_copy(row, owned).start()

                @pl.when(owner - 1 != lon)
                def _():
                    chunk_copy(row, owned, lat, owner - 1, 1).start()

    for l in range(2):
        x = x_ref.at[l]
        for k in range(49):
            for g in range(groups):
                wb_ref[k, g] = jnp.broadcast_to(dw_ref[l, k : k + 1, 128 * g : 128 * g + 128], (8, 128))

        for copy in edge_copies(l, 0, height):
            copy.wait()

        @pl.loop(0, height // 8)
        def _(i):
            part = pl.ds(pl.multiple_of(i * 32, 32), 32)
            place = pl.ds(3 + i * 8, 8)
            after = edge_in[l, 0, part].astype(F32).reshape(4, 8, channels)
            before = edge_in[l, 1, part].astype(F32).reshape(4, 8, channels)
            after = jnp.stack([after, swap_halves(after)], 1).reshape(8, 8, channels)
            before = jnp.stack([swap_halves(before), before], 1).reshape(8, 8, channels)
            for g in range(groups):
                lanes = slice(128 * g, 128 * g + 128)
                x[g, place, COL0 + width : COL0 + width + 8, :] = after[:, :, lanes]
                x[g, place, 0:8, :] = before[:, :, lanes]

        for k, present in enumerate((has_up, has_down)):
            receives = (has_down, has_up)[k]
            place = height + 3 if k == 0 else 0

            @pl.when(present)
            def _():
                for copy in row_copies(l, k):
                    copy.wait_send()

            @pl.when(receives)
            def _():
                for copy in row_copies(l, k):
                    copy.wait_recv()
                middle = row_in[l, k].astype(F32)
                after = corner_in[l, k, 0].astype(F32).reshape(2, 8, channels)
                before = corner_in[l, k, 1].astype(F32).reshape(2, 8, channels)
                for g in range(groups):
                    lanes = slice(128 * g, 128 * g + 128)
                    x[g, place : place + 3, COL0 : COL0 + width, :] = middle[:, :, lanes]
                    for r in range(3):
                        n = r if k == 0 else r + 1
                        right_part = after[n // 2, :, lanes]
                        left_part = before[n // 2, :, lanes]
                        if n % 2:
                            right_part = swap_halves(right_part)
                        else:
                            left_part = swap_halves(left_part)
                        x[g, place + r, COL0 + width : COL0 + width + 8, :] = right_part
                        x[g, place + r, 0:8, :] = left_part

            @pl.when(jnp.logical_not(receives))
            def _():
                for g in range(groups):
                    x[g, place : place + 3] = jnp.zeros((3, width + 16, 128), F32)

        @pl.loop(0, blocks)
        def _(step):
            i = step if l == 0 else lax.rem(step + lon, blocks)

            @pl.loop(0, 2)
            def _(s):
                tile = jnp.where(s == 0, first_tile, second_tile)
                depthwise_block(x, wb_ref, dwb_ref.at[l], d_ref.at[s], tile * TS + i * rows, rows, groups)

            @pl.loop(0, 2)
            def _(s):
                depth = jnp.concatenate([d_ref[s, g].reshape(rows * width, 128) for g in range(groups)], 1)
                u_ref[s] = mix_block(depth, gain_ref[l], shift_ref[l], win_ref[l], bin_ref[l], wout_ref[l],
                                     bout_ref[l]).reshape(rows, width, channels)

            for t in range(3):
                row0 = pl.multiple_of(t * TS + i * rows, rows)
                place = pl.ds(3 + row0, rows)
                for g in range(groups):
                    lanes = slice(128 * g, 128 * g + 128)
                    if t == 1:
                        update = jnp.where(m0 == 0, u_ref[0, :, :, lanes], u_ref[1, :, :, lanes])
                    else:
                        update = u_ref[t // 2, :, :, lanes]
                    field = x[g, place, COL0 : COL0 + width, :]
                    field = (field + (masks[t] * scale_ref[l][:, lanes]) * update).astype(BF16)
                    out_ref[pl.ds(row0, rows), :, lanes] = field
                    if l == 0:
                        x_ref[1, g, place, COL0 : COL0 + width, :] = field.astype(F32)
            if l == 0:
                for t in range(3):
                    row0 = pl.multiple_of(t * TS + i * rows, rows)
                    low = out_ref[pl.ds(row0, rows), 0:16, :].astype(F32)[:, 0:8]
                    high = out_ref[pl.ds(row0, rows), width - 16 : width, :].astype(F32)[:, 8:16]
                    packed = pack_edges(low, high)
                    for k in range(2):
                        edge_out[1, k, pl.ds(pl.multiple_of(row0 * 4, 32), rows * 4)] = packed[k]
                    for copy in edge_copies(1, row0, rows):
                        copy.start()
            else:
                @pl.loop(0, 3 * rows)
                def _(n):
                    t = n // rows
                    send_row(t * TS + i * rows + n - t * rows)

        if l == 0:
            row_out[1, 0] = out_ref[0:3]
            row_out[1, 1] = out_ref[height - 3 : height]
            for k, present in enumerate((has_up, has_down)):
                @pl.when(present)
                def _():
                    for copy in row_copies(1, k):
                        copy.start()

    far = (nlon - 1) * width

    def count_wait(which, sem, n):
        copy = pltpu.make_async_copy(y_ref.at[owned, pl.ds(0, n * width)], y_ref.at[owned, pl.ds(0, n * width)],
                                     group_sems.at[which, sem])
        copy.wait()

    for which in range(2):
        pltpu.make_async_copy(y_ref.at[pl.ds(0, owned), pl.ds(0, far)], y_ref.at[pl.ds(0, owned), pl.ds(0, far)],
                              group_sems.at[which, 0]).wait()
    last = lon == nlon - 1
    sent = nlon - 2 + jnp.where(last, 1, 0) + jnp.where(has_up, 1, 0)
    for n in (nlon - 2, nlon - 1, nlon):
        @pl.when(sent == n)
        def _():
            count_wait(0, 1, n)

    @pl.when(jnp.logical_not(last))
    def _():
        count_wait(1, 1, nlon - 1)

    @pl.when(jnp.logical_and(last, has_down))
    def _():
        count_wait(1, 1, nlon)

    for slot in range(owned):
        own_copy(slot, slot).wait()

    @pl.when(jnp.logical_not(last))
    def _():
        own_copy(0, owned).wait()


def section_call(tiles, coarse, dw, dwb, gain, shift, win, b_in, wout, bout, scale, rows=8):
    height, width, channels = coarse.shape
    groups = channels // 128
    nlon = lax.axis_size("lon")
    owned = height // nlon
    vmem = pl.BlockSpec(memory_space=pltpu.VMEM)
    dma = pltpu.SemaphoreType.DMA
    return pl.pallas_call(
        section_kernel,
        out_shape=jax.ShapeDtypeStruct((owned + 1, nlon * width, channels), BF16),
        in_specs=[pl.BlockSpec(memory_space=pltpu.SMEM)] + [vmem] * 10,
        out_specs=pl.BlockSpec(memory_space=pl.ANY),
        scratch_shapes=[
            pltpu.VMEM((2, groups, height + 6, width + 16, 128), F32),
            pltpu.VMEM((49, groups, 8, 128), F32),
            pltpu.VMEM((2, groups, rows, width, 128), F32),
            pltpu.VMEM((2, rows, width, channels), F32),
            pltpu.VMEM((height, width, channels), BF16),
            pltpu.VMEM((2, 2, height * 4, channels), BF16),
            pltpu.VMEM((2, 2, height * 4, channels), BF16),
            pltpu.VMEM((2, 2, 3, width, channels), BF16),
            pltpu.VMEM((2, 2, 3, width, channels), BF16),
            pltpu.VMEM((2, 2, 2, 16, channels), BF16),
            dma((2, 8)),
            dma((2, 8)),
            dma((owned + 1,)),
            dma((2, 2)),
        ],
        compiler_params=pltpu.CompilerParams(
            collective_id=0, has_side_effects=True, vmem_limit_bytes=50 * 1024 * 1024),
        cost_estimate=pl.CostEstimate(flops=12_000_000_000, bytes_accessed=10_000_000, transcendentals=0),
    )(tiles, coarse, dw, dwb, gain, shift, win, b_in, wout, bout, scale)


UCH = 512


def nt(w, y):
    return lax.dot_general(w, y, (((1,), (1,)), ((), ())), preferred_element_type=F32)


def upsample_kernel(valid_ref, y_ref, next_ref, wt_ref, bias_ref, out_ref):
    width_out = out_ref.shape[1]
    row = lax.broadcasted_iota(jnp.int32, (256, 256), 0)
    col = lax.broadcasted_iota(jnp.int32, (256, 256), 1)
    order = jnp.where(row == (col % 2) * 128 + col // 2, 1.0, 0.0).astype(BF16)
    direct, beside = [], []
    for i in range(4):
        cur, after = y_ref[i], next_ref[i]
        if i == 3:
            valid = valid_ref[0] != 0
            cur = jnp.where(valid, cur, jnp.zeros_like(cur))
            after = jnp.where(valid, after, jnp.zeros_like(after))
        both = jnp.concatenate([cur, after], 0).astype(F32)
        right = both[1 : 1 + UCH].astype(BF16)
        begin, end = (4 if i == 3 else 0, 4 if i == 0 else 6)
        values = nt(wt_ref[begin * width_out : end * width_out], cur)
        direct.append({begin + n: values[n * width_out : (n + 1) * width_out] for n in range(end - begin)})
        begin, end = (8 if i == 3 else 6, 8 if i == 0 else 9)
        values = nt(wt_ref[begin * width_out : end * width_out], right)
        beside.append({begin + n: values[n * width_out : (n + 1) * width_out] for n in range(end - begin)})
    bias = bias_ref[...]
    for i in range(3):
        ee = direct[i][0] + bias
        eo = direct[i][1] + beside[i][6] + bias
        oe = direct[i][2] + direct[i + 1][4] + bias
        oo = direct[i][3] + beside[i][7] + direct[i + 1][5] + beside[i + 1][8] + bias
        for p, (even, odd) in enumerate(((ee, eo), (oe, oo))):
            even, odd = even.astype(BF16), odd.astype(BF16)
            for k in range(UCH // 128):
                lanes = slice(128 * k, 128 * k + 128)
                pair = jnp.concatenate([even[:, lanes], odd[:, lanes]], 1)
                out_ref[2 * i + p, :, 256 * k : 256 * k + 256] = jnp.dot(
                    pair, order, preferred_element_type=F32).astype(BF16)


def upsample_call(valid, y, weight, bias):
    rows, width, channels = y.shape
    out_width = weight.shape[3]
    wt = weight.transpose(0, 1, 3, 2).reshape(9, out_width, channels)
    wt = jnp.concatenate([wt[4:6], wt[7:9], wt[1:3], wt[3:4], wt[6:7], wt[0:1]]).reshape(-1, channels)
    chunks = width // UCH
    bias = jnp.broadcast_to(bias.reshape(-1, 1), (out_width, UCH))
    whole = lambda w: pl.BlockSpec(w.shape, lambda j: (0,) * w.ndim)
    out = pl.pallas_call(
        upsample_kernel,
        grid=(chunks,),
        out_shape=jax.ShapeDtypeStruct((2 * rows - 2, out_width, 2 * width), BF16),
        in_specs=[
            pl.BlockSpec(memory_space=pltpu.SMEM),
            pl.BlockSpec((rows, UCH, channels), lambda j: (0, j, 0)),
            pl.BlockSpec((rows, 16, channels), lambda j: (0, ((j + 1) % chunks) * (UCH // 16), 0)),
            whole(wt), whole(bias),
        ],
        out_specs=pl.BlockSpec((2 * rows - 2, out_width, 2 * UCH), lambda j: (0, 0, j)),
        compiler_params=pltpu.CompilerParams(vmem_limit_bytes=48 * 1024 * 1024),
    )(valid, y, y, wt, bias)
    return out.transpose(0, 2, 1)


def local(coarse, ocean_tiles, dw_weight, dw_bias, norm_gain, norm_shift, in_weight, in_bias,
          out_weight, out_bias, layer_scale, up_weight, up_bias):
    channels = coarse.shape[2]
    row = lambda v: v[:, None, :]
    rows = section_call(ocean_tiles, coarse, dw_weight.reshape(2, 49, channels),
                        dw_bias.reshape(2, channels // 128, 1, 128), row(norm_gain), row(norm_shift), in_weight,
                        row(in_bias), out_weight, row(out_bias), row(layer_scale))
    end = jnp.logical_and(lax.axis_index("lat") == lax.axis_size("lat") - 1,
                          lax.axis_index("lon") == lax.axis_size("lon") - 1)
    valid = jnp.where(end, 0, 1).astype(jnp.int32).reshape(1)
    return upsample_call(valid, rows, up_weight, up_bias)


def solution(mesh):
    placed = (P("lat", "lon", None), P("lat", "lon")) + (P(),) * 11
    return jax.shard_map(
        local, mesh=mesh, in_specs=placed, out_specs=P(("lat", "lon"), None, None), check_vma=False
    )
```

```python
import jax
import jax.numpy as jnp
from jax import lax
from jax.experimental import pallas as pl
from jax.experimental.pallas import tpu as pltpu
from jax.sharding import PartitionSpec as P

TS = 32
COL0 = 8
MESH = pl.DeviceIdType.MESH
F32 = jnp.float32
BF16 = jnp.bfloat16


def depthwise_block(x_ref, wb_ref, bias_ref, l, d_ref, row0, rows, groups, parts):
    for g in range(groups):
        for cb in parts:
            total = jnp.zeros((rows, 8, 128), F32)
            for b in range(7):
                start = COL0 - 3 + b + 8 * cb
                window = x_ref[g, pl.ds(row0, rows + 6), start : start + 8, :]
                for a in range(7):
                    total = total + window[a : a + rows] * wb_ref[a * 7 + b, g]
            d_ref[g, :, 8 * cb : 8 * cb + 8, :] = total + bias_ref[l : l + 1, 128 * g : 128 * g + 128]


def mix_block(depth, gain, shift, w_in, b_in, w_out, b_out):
    center = jnp.mean(depth, -1, keepdims=True)
    offset = depth - center
    spread = jnp.mean(offset * offset, -1, keepdims=True)
    normed = (offset * lax.rsqrt(spread + 1e-06) * gain + shift).astype(BF16)
    hidden = jnp.dot(normed, w_in, preferred_element_type=F32) + b_in
    inner = hidden * (0.7978845608028654 + 0.035677408136300125 * (hidden * hidden))
    half = 0.5 * hidden
    hidden = (half + half * jnp.tanh(inner)).astype(BF16)
    return jnp.dot(hidden, w_out, preferred_element_type=F32) + b_out


def swap_halves(v):
    return jnp.concatenate([v[..., 4:, :], v[..., :4, :]], -2)


def first_half(shape):
    return lax.broadcasted_iota(jnp.int32, shape, len(shape) - 2) < 4


def pack_edges(low, high):
    rows, _, channels = low.shape
    low = low.reshape(rows // 2, 2, 8, channels)
    high = high.reshape(rows // 2, 2, 8, channels)
    pick = first_half((rows // 2, 8, channels))
    left = jnp.where(pick, low[:, 0], swap_halves(low[:, 1]))
    right = jnp.where(pick, swap_halves(high[:, 0]), high[:, 1])
    return [v.reshape(rows * 4, channels).astype(BF16) for v in (left, right)]


def section_kernel(tiles_ref, coarse_ref, dw_ref, dwb_ref, gain_ref, shift_ref, win_ref, bin_ref, wout_ref,
                   bout_ref, scale_ref, y_ref, x_ref, wb_ref, d_ref, u_ref, out_ref, edge_out, edge_in,
                   row_out, row_in, corner_in, halo_send, halo_recv, sems, group_sems):
    height, width, channels = coarse_ref.shape
    groups = channels // 128
    lat, lon = lax.axis_index("lat"), lax.axis_index("lon")
    nlat, nlon = lax.axis_size("lat"), lax.axis_size("lon")
    left, right = lax.rem(lon + nlon - 1, nlon), lax.rem(lon + 1, nlon)
    has_up, has_down = lat > 0, lat < nlat - 1
    owned = height // nlon
    rows = u_ref.shape[1]
    blocks = TS // rows

    barrier = pltpu.get_barrier_semaphore()

    def greet(a, b):
        pl.semaphore_signal(barrier, inc=1, device_id=(a, b), device_id_type=MESH)

    @pl.loop(1, nlon)
    def _(k):
        greet(lat, lax.rem(lon + k, nlon))

    for present, other in ((has_up, lat - 1), (has_down, lat + 1)):
        @pl.when(present)
        def _():
            for b in (left, lon, right):
                greet(other, b)

    @pl.when(jnp.logical_and(has_down, lon == nlon - 1))
    def _():
        @pl.loop(0, nlon)
        def _(k):
            greet(lat + 1, k)

    def edge_copies(l, row0, count):
        part = pl.ds(pl.multiple_of(row0 * 4, 16), count * 4)
        return [pltpu.make_async_remote_copy(
            src_ref=edge_out.at[l, k, part], dst_ref=edge_in.at[l, k, part],
            send_sem=halo_send.at[l, k], recv_sem=halo_recv.at[l, k],
            device_id=(lat, (left, right)[k]), device_id_type=MESH) for k in range(2)]

    def row_copies(l, k):
        other = lat - 1 if k == 0 else lat + 1
        part = pl.ds(0, 16) if k == 0 else pl.ds(height * 4 - 16, 16)
        copies = [pltpu.make_async_remote_copy(
            src_ref=row_out.at[l, k], dst_ref=row_in.at[l, k],
            send_sem=halo_send.at[l, 2 + k], recv_sem=halo_recv.at[l, 2 + k],
            device_id=(other, lon), device_id_type=MESH)]
        for e in range(2):
            copies.append(pltpu.make_async_remote_copy(
                src_ref=edge_out.at[l, e, part], dst_ref=corner_in.at[l, k, e],
                send_sem=halo_send.at[l, 4 + 2 * k + e], recv_sem=halo_recv.at[l, 4 + 2 * k + e],
                device_id=(other, (left, right)[e]), device_id_type=MESH))
        return copies

    m0, m1, m2 = tiles_ref[0, 0], tiles_ref[0, 1], tiles_ref[0, 2]
    first_tile = jnp.where(m0 != 0, 0, 1)
    second_tile = jnp.where(m2 != 0, 2, 1)
    masks = [m.astype(F32) for m in (m0, m1, m2)]

    @pl.loop(0, height // 8)
    def _(i):
        part = pl.ds(pl.multiple_of(i * 8, 8), 8)
        low = coarse_ref[part, 0:16, :].astype(F32)[:, 0:8]
        high = coarse_ref[part, width - 16 : width, :].astype(F32)[:, 8:16]
        packed = pack_edges(low, high)
        for k in range(2):
            edge_out[0, k, pl.ds(pl.multiple_of(i * 32, 32), 32)] = packed[k]

    row_out[0, 0] = coarse_ref[0:3]
    row_out[0, 1] = coarse_ref[height - 3 : height]

    pl.semaphore_wait(barrier, nlon - 1 + jnp.where(has_up, 4, 0) + jnp.where(has_down, 3, 0))
    for k, present in enumerate((has_up, has_down)):
        @pl.when(present)
        def _():
            for copy in row_copies(0, k):
                copy.start()
    for copy in edge_copies(0, 0, height):
        copy.start()

    @pl.loop(0, height // 8)
    def _(i):
        part = pl.ds(pl.multiple_of(i * 8, 8), 8)
        for g in range(groups):
            x_ref[0, g, pl.ds(i * 8 + 3, 8), COL0 : COL0 + width, :] = coarse_ref[
                part, :, 128 * g : 128 * g + 128].astype(F32)

    def chunk_copy(row, slot, a, b, which):
        return pltpu.make_async_remote_copy(
            src_ref=out_ref.at[row], dst_ref=y_ref.at[slot, pl.ds(pl.multiple_of(lon * width, 32), width)],
            send_sem=group_sems.at[0, which], recv_sem=group_sems.at[1, which],
            device_id=(a, b), device_id_type=MESH)

    def own_copy(row, slot):
        return pltpu.make_async_copy(
            out_ref.at[row], y_ref.at[slot, pl.ds(pl.multiple_of(lon * width, 32), width)], sems.at[slot])

    def send_row(row):
        owner = row // owned
        slot = row - owner * owned

        @pl.when(owner == lon)
        def _():
            own_copy(row, slot).start()

        @pl.when(owner != lon)
        def _():
            chunk_copy(row, slot, lat, owner, 0).start()

        @pl.when(slot == 0)
        def _():
            @pl.when(row == 0)
            def _():
                @pl.when(has_up)
                def _():
                    chunk_copy(row, owned, lat - 1, nlon - 1, 1).start()

            @pl.when(row > 0)
            def _():
                @pl.when(owner - 1 == lon)
                def _():
                    own_copy(row, owned).start()

                @pl.when(owner - 1 != lon)
                def _():
                    chunk_copy(row, owned, lat, owner - 1, 1).start()

    for l in range(2):
        x = x_ref.at[l]
        one = slice(l, l + 1)
        for k in range(49):
            for g in range(groups):
                wb_ref[k, g] = jnp.broadcast_to(dw_ref[k // 7, k % 7, l : l + 1, 128 * g : 128 * g + 128], (8, 128))

        def place_edges():
            for copy in edge_copies(l, 0, height):
                copy.wait()

            @pl.loop(0, height // 8)
            def _(i):
                part = pl.ds(pl.multiple_of(i * 32, 32), 32)
                place = pl.ds(3 + i * 8, 8)
                after = edge_in[l, 0, part].astype(F32).reshape(4, 8, channels)
                before = edge_in[l, 1, part].astype(F32).reshape(4, 8, channels)
                after = jnp.stack([after, swap_halves(after)], 1).reshape(8, 8, channels)
                before = jnp.stack([swap_halves(before), before], 1).reshape(8, 8, channels)
                for g in range(groups):
                    lanes = slice(128 * g, 128 * g + 128)
                    x[g, place, COL0 + width : COL0 + width + 8, :] = after[:, :, lanes]
                    x[g, place, 0:8, :] = before[:, :, lanes]

        if l == 1:
            place_edges()

        for k, present in enumerate((has_up, has_down)):
            receives = (has_down, has_up)[k]
            place = height + 3 if k == 0 else 0

            @pl.when(present)
            def _():
                for copy in row_copies(l, k):
                    copy.wait_send()

            @pl.when(receives)
            def _():
                for copy in row_copies(l, k):
                    copy.wait_recv()
                middle = row_in[l, k].astype(F32)
                after = corner_in[l, k, 0].astype(F32).reshape(2, 8, channels)
                before = corner_in[l, k, 1].astype(F32).reshape(2, 8, channels)
                for g in range(groups):
                    lanes = slice(128 * g, 128 * g + 128)
                    x[g, place : place + 3, COL0 : COL0 + width, :] = middle[:, :, lanes]
                    for r in range(3):
                        n = r if k == 0 else r + 1
                        right_part = after[n // 2, :, lanes]
                        left_part = before[n // 2, :, lanes]
                        if n % 2:
                            right_part = swap_halves(right_part)
                        else:
                            left_part = swap_halves(left_part)
                        x[g, place + r, COL0 + width : COL0 + width + 8, :] = right_part
                        x[g, place + r, 0:8, :] = left_part

            @pl.when(jnp.logical_not(receives))
            def _():
                for g in range(groups):
                    x[g, place : place + 3] = jnp.zeros((3, width + 16, 128), F32)

        def depthwise(i, parts):
            @pl.loop(0, 2)
            def _(s):
                tile = jnp.where(s == 0, first_tile, second_tile)
                depthwise_block(x, wb_ref, dwb_ref, l, d_ref.at[s, :, pl.ds(pl.multiple_of(i * rows, rows), rows)],
                                tile * TS + i * rows, rows, groups, parts)

        if l == 0:
            @pl.loop(0, blocks)
            def _(i):
                depthwise(i, (1, 2))

            place_edges()

        @pl.loop(0, blocks)
        def _(step):
            i = step if l == 0 else lax.rem(step + lon // 8, blocks)

            depthwise(i, (0, 3) if l == 0 else (0, 1, 2, 3))

            @pl.loop(0, 2)
            def _(s):
                depth = jnp.concatenate([d_ref[s, g, pl.ds(pl.multiple_of(i * rows, rows), rows)].reshape(rows * width, 128) for g in range(groups)], 1)
                u_ref[s] = mix_block(depth, gain_ref[one], shift_ref[one], win_ref[l], bin_ref[one], wout_ref[l],
                                     bout_ref[one]).reshape(rows, width, channels)

            for t in range(3):
                row0 = pl.multiple_of(t * TS + i * rows, rows)
                place = pl.ds(3 + row0, rows)
                for g in range(groups):
                    lanes = slice(128 * g, 128 * g + 128)
                    if t == 1:
                        update = jnp.where(m0 == 0, u_ref[0, :, :, lanes], u_ref[1, :, :, lanes])
                    else:
                        update = u_ref[t // 2, :, :, lanes]
                    field = x[g, place, COL0 : COL0 + width, :]
                    field = (field + (masks[t] * scale_ref[one, lanes]) * update).astype(BF16)
                    out_ref[pl.ds(row0, rows), :, lanes] = field
                    if l == 0:
                        x_ref[1, g, place, COL0 : COL0 + width, :] = field.astype(F32)
            if l == 0:
                for t in range(3):
                    row0 = pl.multiple_of(t * TS + i * rows, rows)
                    low = out_ref[pl.ds(row0, rows), 0:16, :].astype(F32)[:, 0:8]
                    high = out_ref[pl.ds(row0, rows), width - 16 : width, :].astype(F32)[:, 8:16]
                    packed = pack_edges(low, high)
                    for k in range(2):
                        edge_out[1, k, pl.ds(pl.multiple_of(row0 * 4, 32), rows * 4)] = packed[k]
                    for copy in edge_copies(1, row0, rows):
                        copy.start()
            else:
                @pl.loop(0, 3 * rows)
                def _(n):
                    t = lax.rem(n, 3)
                    r = lax.rem(n // 3 * 5 + lon // 4, rows)
                    send_row(t * TS + i * rows + r)

        if l == 0:
            row_out[1, 0] = out_ref[0:3]
            row_out[1, 1] = out_ref[height - 3 : height]
            for k, present in enumerate((has_up, has_down)):
                @pl.when(present)
                def _():
                    for copy in row_copies(1, k):
                        copy.start()

    far = (nlon - 1) * width

    def count_wait(which, sem, n):
        copy = pltpu.make_async_copy(y_ref.at[owned, pl.ds(0, n * width)], y_ref.at[owned, pl.ds(0, n * width)],
                                     group_sems.at[which, sem])
        copy.wait()

    for which in range(2):
        pltpu.make_async_copy(y_ref.at[pl.ds(0, owned), pl.ds(0, far)], y_ref.at[pl.ds(0, owned), pl.ds(0, far)],
                              group_sems.at[which, 0]).wait()
    last = lon == nlon - 1
    sent = nlon - 2 + jnp.where(last, 1, 0) + jnp.where(has_up, 1, 0)
    for n in (nlon - 2, nlon - 1, nlon):
        @pl.when(sent == n)
        def _():
            count_wait(0, 1, n)

    @pl.when(jnp.logical_not(last))
    def _():
        count_wait(1, 1, nlon - 1)

    @pl.when(jnp.logical_and(last, has_down))
    def _():
        count_wait(1, 1, nlon)

    for slot in range(owned):
        own_copy(slot, slot).wait()

    @pl.when(jnp.logical_not(last))
    def _():
        own_copy(0, owned).wait()


def section_call(tiles, coarse, dw, dwb, gain, shift, win, b_in, wout, bout, scale, rows=8):
    height, width, channels = coarse.shape
    groups = channels // 128
    nlon = lax.axis_size("lon")
    owned = height // nlon
    vmem = pl.BlockSpec(memory_space=pltpu.VMEM)
    dma = pltpu.SemaphoreType.DMA
    return pl.pallas_call(
        section_kernel,
        out_shape=jax.ShapeDtypeStruct((owned + 1, nlon * width, channels), BF16),
        in_specs=[pl.BlockSpec(memory_space=pltpu.SMEM)] + [vmem] * 10,
        out_specs=pl.BlockSpec(memory_space=pl.ANY),
        scratch_shapes=[
            pltpu.VMEM((2, groups, height + 6, width + 16, 128), F32),
            pltpu.VMEM((49, groups, 8, 128), F32),
            pltpu.VMEM((2, groups, TS, width, 128), F32),
            pltpu.VMEM((2, rows, width, channels), F32),
            pltpu.VMEM((height, width, channels), BF16),
            pltpu.VMEM((2, 2, height * 4, channels), BF16),
            pltpu.VMEM((2, 2, height * 4, channels), BF16),
            pltpu.VMEM((2, 2, 3, width, channels), BF16),
            pltpu.VMEM((2, 2, 3, width, channels), BF16),
            pltpu.VMEM((2, 2, 2, 16, channels), BF16),
            dma((2, 8)),
            dma((2, 8)),
            dma((owned + 1,)),
            dma((2, 2)),
        ],
        compiler_params=pltpu.CompilerParams(
            collective_id=0, has_side_effects=True, vmem_limit_bytes=60 * 1024 * 1024),
        cost_estimate=pl.CostEstimate(flops=12_000_000_000, bytes_accessed=10_000_000, transcendentals=0),
    )(tiles, coarse, dw, dwb, gain, shift, win, b_in, wout, bout, scale)


UCH = 512


def nt(w, y):
    return lax.dot_general(w, y, (((1,), (1,)), ((), ())), preferred_element_type=F32)


TAPS = (4, 5, 7, 8, 1, 2, 3, 6, 0)


def upsample_kernel(y_ref, next_ref, wt_ref, bias_ref, out_ref):
    last = jnp.logical_and(lax.axis_index("lat") == lax.axis_size("lat") - 1,
                           lax.axis_index("lon") == lax.axis_size("lon") - 1)
    valid = jnp.logical_not(last)

    def weights(begin, end):
        return jnp.concatenate([wt_ref[n] for n in TAPS[begin:end]], 0)

    width_out = out_ref.shape[1]
    row = lax.broadcasted_iota(jnp.int32, (256, 256), 0)
    col = lax.broadcasted_iota(jnp.int32, (256, 256), 1)
    order = jnp.where(row == (col % 2) * 128 + col // 2, 1.0, 0.0).astype(BF16)
    direct, beside = [], []
    for i in range(4):
        cur, after = y_ref[i], next_ref[i]
        if i == 3:
            cur = jnp.where(valid, cur, jnp.zeros_like(cur))
            after = jnp.where(valid, after, jnp.zeros_like(after))
        both = jnp.concatenate([cur, after], 0).astype(F32)
        right = both[1 : 1 + UCH].astype(BF16)
        begin, end = (4 if i == 3 else 0, 4 if i == 0 else 6)
        values = nt(weights(begin, end), cur)
        direct.append({begin + n: values[n * width_out : (n + 1) * width_out] for n in range(end - begin)})
        begin, end = (8 if i == 3 else 6, 8 if i == 0 else 9)
        values = nt(weights(begin, end), right)
        beside.append({begin + n: values[n * width_out : (n + 1) * width_out] for n in range(end - begin)})
    same = lax.broadcasted_iota(jnp.int32, (width_out, width_out), 0) == lax.broadcasted_iota(
        jnp.int32, (width_out, width_out), 1)
    bias = jnp.sum(jnp.where(same, bias_ref[...], 0.0), axis=1, keepdims=True)
    for i in range(3):
        ee = direct[i][0] + bias
        eo = direct[i][1] + beside[i][6] + bias
        oe = direct[i][2] + direct[i + 1][4] + bias
        oo = direct[i][3] + beside[i][7] + direct[i + 1][5] + beside[i + 1][8] + bias
        for p, (even, odd) in enumerate(((ee, eo), (oe, oo))):
            even, odd = even.astype(BF16), odd.astype(BF16)
            for k in range(UCH // 128):
                lanes = slice(128 * k, 128 * k + 128)
                pair = jnp.concatenate([even[:, lanes], odd[:, lanes]], 1)
                out_ref[2 * i + p, :, 256 * k : 256 * k + 256] = jnp.dot(
                    pair, order, preferred_element_type=F32).astype(BF16)


def upsample_call(y, weight, bias):
    rows, width, channels = y.shape
    out_width = weight.shape[3]
    wt = weight.transpose(0, 1, 3, 2).reshape(9, out_width, channels)
    chunks = width // UCH
    bias = bias.reshape(1, -1)
    whole = lambda w: pl.BlockSpec(w.shape, lambda j: (0,) * w.ndim)
    out = pl.pallas_call(
        upsample_kernel,
        grid=(chunks,),
        out_shape=jax.ShapeDtypeStruct((2 * rows - 2, out_width, 2 * width), BF16),
        in_specs=[
            pl.BlockSpec((rows, UCH, channels), lambda j: (0, j, 0)),
            pl.BlockSpec((rows, 16, channels), lambda j: (0, ((j + 1) % chunks) * (UCH // 16), 0)),
            whole(wt), whole(bias),
        ],
        out_specs=pl.BlockSpec((2 * rows - 2, out_width, 2 * UCH), lambda j: (0, 0, j)),
        compiler_params=pltpu.CompilerParams(vmem_limit_bytes=60 * 1024 * 1024),
    )(y, y, wt, bias)
    return out.transpose(0, 2, 1)


def local(coarse, ocean_tiles, dw_weight, dw_bias, norm_gain, norm_shift, in_weight, in_bias,
          out_weight, out_bias, layer_scale, up_weight, up_bias):
    rows = section_call(ocean_tiles.T, coarse, dw_weight.transpose(1, 2, 0, 3), dw_bias, norm_gain, norm_shift,
                        in_weight, in_bias, out_weight, out_bias, layer_scale)
    return upsample_call(rows, up_weight, up_bias)


def solution(mesh):
    placed = (P("lat", "lon", None), P("lat", "lon")) + (P(),) * 11
    return jax.shard_map(
        local, mesh=mesh, in_specs=placed, out_specs=P(("lat", "lon"), None, None), check_vma=False
    )
```

```python
import functools
import jax
import jax.numpy as jnp
from jax import lax
from jax.experimental import pallas as pl
from jax.experimental.pallas import tpu as pltpu
from jax.sharding import PartitionSpec as P

TS = 32
COL0 = 8
MESH = pl.DeviceIdType.MESH
F32 = jnp.float32
BF16 = jnp.bfloat16


def depthwise_block(x_ref, wb_ref, bias_ref, l, d_ref, row0, rows, groups, parts):
    for g in range(groups):
        for cb in parts:
            total = jnp.zeros((rows, 8, 128), F32)
            for b in range(7):
                start = COL0 - 3 + b + 8 * cb
                window = x_ref[g, pl.ds(row0, rows + 6), start : start + 8, :]
                for a in range(7):
                    total = total + window[a : a + rows] * wb_ref[a * 7 + b, g]
            d_ref[g, :, 8 * cb : 8 * cb + 8, :] = total + bias_ref[l : l + 1, 128 * g : 128 * g + 128]


def mix_block(depth, gain, shift, w_in, b_in, w_out, b_out):
    center = jnp.mean(depth, -1, keepdims=True)
    offset = depth - center
    spread = jnp.mean(offset * offset, -1, keepdims=True)
    normed = (offset * lax.rsqrt(spread + 1e-06) * gain + shift).astype(BF16)
    hidden = jnp.dot(normed, w_in, preferred_element_type=F32) + b_in
    inner = hidden * (0.7978845608028654 + 0.035677408136300125 * (hidden * hidden))
    half = 0.5 * hidden
    hidden = (half + half * jnp.tanh(inner)).astype(BF16)
    return jnp.dot(hidden, w_out, preferred_element_type=F32) + b_out


CHUNK = 80


def turned(v, shift):
    return pltpu.roll(v, shift % 8, axis=0) if shift % 8 else v


def pack_rows(lines, base):
    place = lax.broadcasted_iota(jnp.int32, lines[0].shape, 0)
    blocks = []
    for k in range(3):
        block = jnp.zeros_like(lines[0])
        for r in range(8):
            low = 3 * r - 8 * k
            if low > -3 and low < 8:
                inside = jnp.logical_and(place >= low, place < low + 3)
                block = jnp.where(inside, turned(lines[r], low - base), block)
        blocks.append(block)
    return blocks


def unpack_row(blocks, r, base):
    first, last = 3 * r // 8, (3 * r + 2) // 8
    value = turned(blocks[first], base - 3 * r + 8 * first)
    if last != first:
        place = lax.broadcasted_iota(jnp.int32, value.shape, 0)
        other = turned(blocks[last], base - 3 * r + 8 * last)
        value = jnp.where(place >= base + 8 * last - 3 * r, other, value)
    return value


def section_kernel(step_rows, tiles_ref, coarse_hbm, dw_hbm, dwb_ref, gain_ref, shift_ref, win_hbm, bin_ref, wout_hbm,
                   bout_ref, scale_ref, y_ref, coarse_ref, dw_ref, win_ref, wout_ref, load_sems, x_ref, wb_ref, d_ref, u_ref, out_ref, edge_out, edge_in,
                   row_out, row_in, corner_in, halo_send, halo_recv, sems, group_sems):
    height, width, channels = coarse_ref.shape
    groups = channels // 128
    lat, lon = lax.axis_index("lat"), lax.axis_index("lon")
    nlat, nlon = lax.axis_size("lat"), lax.axis_size("lon")
    left, right = lax.rem(lon + nlon - 1, nlon), lax.rem(lon + 1, nlon)
    has_up, has_down = lat > 0, lat < nlat - 1
    owned = height // nlon

    loads = [pltpu.make_async_copy(a, b, load_sems.at[n]) for n, (a, b) in enumerate((
        (coarse_hbm, coarse_ref), (dw_hbm, dw_ref), (win_hbm, win_ref), (wout_hbm, wout_ref)))]
    for load in loads:
        load.start()

    barrier = pltpu.get_barrier_semaphore()

    def greet(a, b):
        pl.semaphore_signal(barrier, inc=1, device_id=(a, b), device_id_type=MESH)

    @pl.loop(1, nlon)
    def _(k):
        greet(lat, lax.rem(lon + k, nlon))

    for present, other in ((has_up, lat - 1), (has_down, lat + 1)):
        @pl.when(present)
        def _():
            for b in (left, lon, right):
                greet(other, b)

    @pl.when(jnp.logical_and(has_down, lon == nlon - 1))
    def _():
        @pl.loop(0, nlon)
        def _(k):
            greet(lat + 1, k)

    def edge_copies(l, chunk, count):
        part = pl.ds(pl.multiple_of(chunk * CHUNK, CHUNK), count * CHUNK)
        return [pltpu.make_async_remote_copy(
            src_ref=edge_out.at[l, k, part], dst_ref=edge_in.at[l, k, part],
            send_sem=halo_send.at[l, k], recv_sem=halo_recv.at[l, k],
            device_id=(lat, (left, right)[k]), device_id_type=MESH) for k in range(2)]

    def pack_edges(source, l, i):
        low, high = [], []
        for t in range(3):
            part = pl.ds(pl.multiple_of(t * TS + i * 8, 8), 8)
            begin = source[part, 0:16, :].astype(F32)
            end = source[part, width - 16 : width, :].astype(F32)
            low += pack_rows([begin[r, 0:8] for r in range(8)], 0)
            high += pack_rows([end[r, 8:16] for r in range(8)], 5)
        for k, blocks in enumerate((low, high)):
            blocks = blocks + [jnp.zeros_like(blocks[0])]
            edge_out[l, k, pl.ds(pl.multiple_of(i * CHUNK, CHUNK), CHUNK)] = jnp.concatenate(blocks, 0).astype(BF16)

    def row_copies(l, k):
        other = lat - 1 if k == 0 else lat + 1
        part = pl.ds(0, 32) if k == 0 else pl.ds(4 * CHUNK - 32, 32)
        copies = [pltpu.make_async_remote_copy(
            src_ref=row_out.at[l, k], dst_ref=row_in.at[l, k],
            send_sem=halo_send.at[l, 2 + k], recv_sem=halo_recv.at[l, 2 + k],
            device_id=(other, lon), device_id_type=MESH)]
        for e in range(2):
            copies.append(pltpu.make_async_remote_copy(
                src_ref=edge_out.at[l, e, part], dst_ref=corner_in.at[l, k, e],
                send_sem=halo_send.at[l, 4 + 2 * k + e], recv_sem=halo_recv.at[l, 4 + 2 * k + e],
                device_id=(other, (left, right)[e]), device_id_type=MESH))
        return copies

    m0, m1, m2 = tiles_ref[0, 0], tiles_ref[0, 1], tiles_ref[0, 2]
    first_tile = jnp.where(m0 != 0, 0, 1)
    second_tile = jnp.where(m2 != 0, 2, 1)
    masks = [m.astype(F32) for m in (m0, m1, m2)]

    loads[0].wait()

    @pl.loop(0, 4)
    def _(i):
        pack_edges(coarse_ref, 0, i)

    row_out[0, 0] = coarse_ref[0:3]
    row_out[0, 1] = coarse_ref[height - 3 : height]

    pl.semaphore_wait(barrier, nlon - 1 + jnp.where(has_up, 4, 0) + jnp.where(has_down, 3, 0))
    for k, present in enumerate((has_up, has_down)):
        @pl.when(present)
        def _():
            for copy in row_copies(0, k):
                copy.start()
    for copy in edge_copies(0, 0, 4):
        copy.start()

    @pl.loop(0, height // 8)
    def _(i):
        part = pl.ds(pl.multiple_of(i * 8, 8), 8)
        for g in range(groups):
            x_ref[0, g, pl.ds(i * 8 + 3, 8), COL0 : COL0 + width, :] = coarse_ref[
                part, :, 128 * g : 128 * g + 128].astype(F32)

    def chunk_copy(row, slot, a, b, which):
        return pltpu.make_async_remote_copy(
            src_ref=out_ref.at[row], dst_ref=y_ref.at[slot, pl.ds(pl.multiple_of(lon * width, 32), width)],
            send_sem=group_sems.at[0, which], recv_sem=group_sems.at[1, which],
            device_id=(a, b), device_id_type=MESH)

    def own_copy(row, slot):
        return pltpu.make_async_copy(
            out_ref.at[row], y_ref.at[slot, pl.ds(pl.multiple_of(lon * width, 32), width)], sems.at[slot])

    def send_row(row):
        owner = row // owned
        slot = row - owner * owned

        @pl.when(owner == lon)
        def _():
            own_copy(row, slot).start()

        @pl.when(owner != lon)
        def _():
            chunk_copy(row, slot, lat, owner, 0).start()

        @pl.when(slot == 0)
        def _():
            @pl.when(row == 0)
            def _():
                @pl.when(has_up)
                def _():
                    chunk_copy(row, owned, lat - 1, nlon - 1, 1).start()

            @pl.when(row > 0)
            def _():
                @pl.when(owner - 1 == lon)
                def _():
                    own_copy(row, owned).start()

                @pl.when(owner - 1 != lon)
                def _():
                    chunk_copy(row, owned, lat, owner - 1, 1).start()

    for load in loads[1:]:
        load.wait()

    for l in range(2):
        x = x_ref.at[l]
        rows = step_rows[l]
        blocks = TS // rows
        one = slice(l, l + 1)
        for k in range(49):
            for g in range(groups):
                wb_ref[k, g] = jnp.broadcast_to(dw_ref[k // 7, k % 7, l : l + 1, 128 * g : 128 * g + 128], (8, 128))

        def place_edges():
            for copy in edge_copies(l, 0, 4):
                copy.wait()

            @pl.loop(0, 4)
            def _(i):
                part = pl.ds(pl.multiple_of(i * CHUNK, CHUNK), CHUNK)
                after = edge_in[l, 0, part].astype(F32)
                before = edge_in[l, 1, part].astype(F32)
                for t in range(3):
                    after_blocks = [after[8 * n : 8 * n + 8] for n in range(3 * t, 3 * t + 3)]
                    before_blocks = [before[8 * n : 8 * n + 8] for n in range(3 * t, 3 * t + 3)]
                    for r in range(8):
                        line = 3 + t * TS + i * 8 + r
                        right_part = unpack_row(after_blocks, r, 0)
                        left_part = unpack_row(before_blocks, r, 5)
                        for g in range(groups):
                            lanes = slice(128 * g, 128 * g + 128)
                            x[g, line, COL0 + width : COL0 + width + 8, :] = right_part[:, lanes]
                            x[g, line, 0:8, :] = left_part[:, lanes]

        def place_rows():
            for k, present in enumerate((has_up, has_down)):
                receives = (has_down, has_up)[k]
                place = height + 3 if k == 0 else 0

                @pl.when(present)
                def _():
                    for copy in row_copies(l, k):
                        copy.wait_send()

                @pl.when(receives)
                def _():
                    for copy in row_copies(l, k):
                        copy.wait_recv()
                    middle = row_in[l, k].astype(F32)
                    after = corner_in[l, k, 0].astype(F32)
                    before = corner_in[l, k, 1].astype(F32)
                    after = [after[8 * n : 8 * n + 8] for n in range(3)]
                    before = [before[8 * n : 8 * n + 8] for n in range(3)]
                    for g in range(groups):
                        lanes = slice(128 * g, 128 * g + 128)
                        x[g, place : place + 3, COL0 : COL0 + width, :] = middle[:, :, lanes]
                        for r in range(3):
                            n = r if k == 0 else r + 5
                            x[g, place + r, COL0 + width : COL0 + width + 8, :] = unpack_row(after, n, 0)[:, lanes]
                            x[g, place + r, 0:8, :] = unpack_row(before, n, 5)[:, lanes]

                @pl.when(jnp.logical_not(receives))
                def _():
                    for g in range(groups):
                        x[g, place : place + 3] = jnp.zeros((3, width + 16, 128), F32)

        if l == 1:
            place_rows()
            place_edges()

        def depthwise(i, parts):
            @pl.loop(0, 2)
            def _(s):
                tile = jnp.where(s == 0, first_tile, second_tile)
                depthwise_block(x, wb_ref, dwb_ref, l, d_ref.at[s, :, pl.ds(pl.multiple_of(i * rows, rows), rows)],
                                tile * TS + i * rows, rows, groups, parts)

        if l == 0:
            @pl.loop(1, blocks - 1)
            def _(i):
                depthwise(i, (1, 2))

            place_rows()

            @pl.loop(0, 2)
            def _(n):
                depthwise(n * (blocks - 1), (1, 2))

            place_edges()

        @pl.loop(0, blocks)
        def _(step):
            if l == 0:
                i = jnp.where(step < 2, step * (blocks - 1), step - 1)
            else:
                i = lax.rem(step + lon // 8 * 2 + 4 * lax.rem(lat, 2), blocks)

            depthwise(i, (0, 3) if l == 0 else (0, 1, 2, 3))

            @pl.loop(0, 2)
            def _(s):
                depth = jnp.concatenate([d_ref[s, g, pl.ds(pl.multiple_of(i * rows, rows), rows)].reshape(rows * width, 128) for g in range(groups)], 1)
                u_ref[s, 0:rows] = mix_block(depth, gain_ref[one], shift_ref[one], win_ref[l], bin_ref[one], wout_ref[l],
                                     bout_ref[one]).reshape(rows, width, channels)

            for t in range(3):
                row0 = pl.multiple_of(t * TS + i * rows, rows)
                place = pl.ds(3 + row0, rows)
                for g in range(groups):
                    lanes = slice(128 * g, 128 * g + 128)
                    if t == 1:
                        update = jnp.where(m0 == 0, u_ref[0, 0:rows, :, lanes], u_ref[1, 0:rows, :, lanes])
                    else:
                        update = u_ref[t // 2, 0:rows, :, lanes]
                    field = x[g, place, COL0 : COL0 + width, :]
                    field = (field + (masks[t] * scale_ref[one, lanes]) * update).astype(BF16)
                    out_ref[pl.ds(row0, rows), :, lanes] = field
                    if l == 0:
                        x_ref[1, g, place, COL0 : COL0 + width, :] = field.astype(F32)
            if l == 0:
                pack_edges(out_ref, 1, i)
                for copy in edge_copies(1, i, 1):
                    copy.start()

                @pl.when(step == 1)
                def _():
                    row_out[1, 0] = out_ref[0:3]
                    row_out[1, 1] = out_ref[height - 3 : height]
                    for k, present in enumerate((has_up, has_down)):
                        @pl.when(present)
                        def _():
                            for copy in row_copies(1, k):
                                copy.start()
            else:
                @pl.loop(0, 3 * rows)
                def _(n):
                    t = lax.rem(n + lat, 3)
                    r = lax.rem(n // 3 * 3 + lon // 2, rows)
                    send_row(t * TS + i * rows + r)

    far = (nlon - 1) * width

    def count_wait(which, sem, n):
        copy = pltpu.make_async_copy(y_ref.at[owned, pl.ds(0, n * width)], y_ref.at[owned, pl.ds(0, n * width)],
                                     group_sems.at[which, sem])
        copy.wait()

    for which in range(2):
        pltpu.make_async_copy(y_ref.at[pl.ds(0, owned), pl.ds(0, far)], y_ref.at[pl.ds(0, owned), pl.ds(0, far)],
                              group_sems.at[which, 0]).wait()
    last = lon == nlon - 1
    sent = nlon - 2 + jnp.where(last, 1, 0) + jnp.where(has_up, 1, 0)
    for n in (nlon - 2, nlon - 1, nlon):
        @pl.when(sent == n)
        def _():
            count_wait(0, 1, n)

    @pl.when(jnp.logical_not(last))
    def _():
        count_wait(1, 1, nlon - 1)

    @pl.when(jnp.logical_and(last, has_down))
    def _():
        count_wait(1, 1, nlon)

    for slot in range(owned):
        own_copy(slot, slot).wait()

    @pl.when(jnp.logical_not(last))
    def _():
        own_copy(0, owned).wait()


def section_call(tiles, coarse, dw, dwb, gain, shift, win, b_in, wout, bout, scale, step_rows=(8, 4)):
    height, width, channels = coarse.shape
    groups = channels // 128
    nlon = lax.axis_size("lon")
    owned = height // nlon
    vmem = pl.BlockSpec(memory_space=pltpu.VMEM)
    hbm = pl.BlockSpec(memory_space=pl.ANY)
    dma = pltpu.SemaphoreType.DMA
    rows = max(step_rows)
    return pl.pallas_call(
        functools.partial(section_kernel, step_rows),
        out_shape=jax.ShapeDtypeStruct((owned + 1, nlon * width, channels), BF16),
        in_specs=[pl.BlockSpec(memory_space=pltpu.SMEM), hbm, hbm, vmem, vmem, vmem, hbm, vmem, hbm, vmem, vmem],
        out_specs=pl.BlockSpec(memory_space=pl.ANY),
        scratch_shapes=[
            pltpu.VMEM(coarse.shape, BF16),
            pltpu.VMEM(dw.shape, F32),
            pltpu.VMEM(win.shape, BF16),
            pltpu.VMEM(wout.shape, BF16),
            dma((4,)),
            pltpu.VMEM((2, groups, height + 6, width + 16, 128), F32),
            pltpu.VMEM((49, groups, 8, 128), F32),
            pltpu.VMEM((2, groups, TS, width, 128), F32),
            pltpu.VMEM((2, rows, width, channels), F32),
            pltpu.VMEM((height, width, channels), BF16),
            pltpu.VMEM((2, 2, 4 * CHUNK, channels), BF16),
            pltpu.VMEM((2, 2, 4 * CHUNK, channels), BF16),
            pltpu.VMEM((2, 2, 3, width, channels), BF16),
            pltpu.VMEM((2, 2, 3, width, channels), BF16),
            pltpu.VMEM((2, 2, 2, 32, channels), BF16),
            dma((2, 8)),
            dma((2, 8)),
            dma((owned + 1,)),
            dma((2, 2)),
        ],
        compiler_params=pltpu.CompilerParams(
            collective_id=0, has_side_effects=True, vmem_limit_bytes=60 * 1024 * 1024),
        cost_estimate=pl.CostEstimate(flops=12_000_000_000, bytes_accessed=10_000_000, transcendentals=0),
    )(tiles, coarse, dw, dwb, gain, shift, win, b_in, wout, bout, scale)


UCH = 512


def nt(w, y):
    return lax.dot_general(w, y, (((1,), (1,)), ((), ())), preferred_element_type=F32)


TAPS = (4, 5, 7, 8, 1, 2, 3, 6, 0)


def upsample_kernel(y_ref, next_ref, wt_ref, bias_ref, out_ref):
    last = jnp.logical_and(lax.axis_index("lat") == lax.axis_size("lat") - 1,
                           lax.axis_index("lon") == lax.axis_size("lon") - 1)
    valid = jnp.logical_not(last)

    def weights(begin, end):
        return jnp.concatenate([wt_ref[n] for n in TAPS[begin:end]], 0)

    width_out = out_ref.shape[1]
    row = lax.broadcasted_iota(jnp.int32, (256, 256), 0)
    col = lax.broadcasted_iota(jnp.int32, (256, 256), 1)
    order = jnp.where(row == (col % 2) * 128 + col // 2, 1.0, 0.0).astype(BF16)
    direct, beside = [], []
    for i in range(4):
        cur, after = y_ref[i], next_ref[i]
        if i == 3:
            cur = jnp.where(valid, cur, jnp.zeros_like(cur))
            after = jnp.where(valid, after, jnp.zeros_like(after))
        both = jnp.concatenate([cur, after], 0).astype(F32)
        right = both[1 : 1 + UCH].astype(BF16)
        begin, end = (4 if i == 3 else 0, 4 if i == 0 else 6)
        values = nt(weights(begin, end), cur)
        direct.append({begin + n: values[n * width_out : (n + 1) * width_out] for n in range(end - begin)})
        begin, end = (8 if i == 3 else 6, 8 if i == 0 else 9)
        values = nt(weights(begin, end), right)
        beside.append({begin + n: values[n * width_out : (n + 1) * width_out] for n in range(end - begin)})
    same = lax.broadcasted_iota(jnp.int32, (width_out, width_out), 0) == lax.broadcasted_iota(
        jnp.int32, (width_out, width_out), 1)
    bias = jnp.sum(jnp.where(same, bias_ref[...], 0.0), axis=1, keepdims=True)
    for i in range(3):
        ee = direct[i][0] + bias
        eo = direct[i][1] + beside[i][6] + bias
        oe = direct[i][2] + direct[i + 1][4] + bias
        oo = direct[i][3] + beside[i][7] + direct[i + 1][5] + beside[i + 1][8] + bias
        for p, (even, odd) in enumerate(((ee, eo), (oe, oo))):
            even, odd = even.astype(BF16), odd.astype(BF16)
            for k in range(UCH // 128):
                lanes = slice(128 * k, 128 * k + 128)
                pair = jnp.concatenate([even[:, lanes], odd[:, lanes]], 1)
                out_ref[2 * i + p, :, 256 * k : 256 * k + 256] = jnp.dot(
                    pair, order, preferred_element_type=F32).astype(BF16)


def upsample_call(y, weight, bias):
    rows, width, channels = y.shape
    out_width = weight.shape[3]
    wt = weight.transpose(0, 1, 3, 2).reshape(9, out_width, channels)
    chunks = width // UCH
    bias = bias.reshape(1, -1)
    whole = lambda w: pl.BlockSpec(w.shape, lambda j: (0,) * w.ndim)
    out = pl.pallas_call(
        upsample_kernel,
        grid=(chunks,),
        out_shape=jax.ShapeDtypeStruct((2 * rows - 2, out_width, 2 * width), BF16),
        in_specs=[
            pl.BlockSpec((rows, UCH, channels), lambda j: (0, j, 0)),
            pl.BlockSpec((rows, 16, channels), lambda j: (0, ((j + 1) % chunks) * (UCH // 16), 0)),
            whole(wt), whole(bias),
        ],
        out_specs=pl.BlockSpec((2 * rows - 2, out_width, 2 * UCH), lambda j: (0, 0, j)),
        compiler_params=pltpu.CompilerParams(vmem_limit_bytes=60 * 1024 * 1024),
    )(y, y, wt, bias)
    return out.transpose(0, 2, 1)


def local(coarse, ocean_tiles, dw_weight, dw_bias, norm_gain, norm_shift, in_weight, in_bias,
          out_weight, out_bias, layer_scale, up_weight, up_bias):
    rows = section_call(ocean_tiles.T, coarse, dw_weight.transpose(1, 2, 0, 3), dw_bias, norm_gain, norm_shift,
                        in_weight, in_bias, out_weight, out_bias, layer_scale)
    return upsample_call(rows, up_weight, up_bias)


def solution(mesh):
    placed = (P("lat", "lon", None), P("lat", "lon")) + (P(),) * 11
    return jax.shard_map(
        local, mesh=mesh, in_specs=placed, out_specs=P(("lat", "lon"), None, None), check_vma=False
    )
```

```python
import functools
import jax
import jax.numpy as jnp
from jax import lax
from jax.experimental import pallas as pl
from jax.experimental.pallas import tpu as pltpu
from jax.sharding import PartitionSpec as P

TS = 32
COL0 = 8
MESH = pl.DeviceIdType.MESH
F32 = jnp.float32
BF16 = jnp.bfloat16


def depthwise_block(x_ref, wb_ref, bias_ref, l, d_ref, row0, rows, groups, parts):
    for g in range(groups):
        for cb in parts:
            total = jnp.zeros((rows, 8, 128), F32)
            for b in range(7):
                start = COL0 - 3 + b + 8 * cb
                window = x_ref[g, pl.ds(row0, rows + 6), start : start + 8, :]
                for a in range(7):
                    total = total + window[a : a + rows] * wb_ref[a * 7 + b, g]
            d_ref[g, :, 8 * cb : 8 * cb + 8, :] = total + bias_ref[l : l + 1, 128 * g : 128 * g + 128]


def mix_block(depth, gain, shift, w_in, b_in, w_out, b_out):
    center = jnp.mean(depth, -1, keepdims=True)
    offset = depth - center
    spread = jnp.mean(offset * offset, -1, keepdims=True)
    normed = (offset * lax.rsqrt(spread + 1e-06) * gain + shift).astype(BF16)
    hidden = jnp.dot(normed, w_in, preferred_element_type=F32) + b_in
    inner = hidden * (0.7978845608028654 + 0.035677408136300125 * (hidden * hidden))
    half = 0.5 * hidden
    hidden = (half + half * jnp.tanh(inner)).astype(BF16)
    return jnp.dot(hidden, w_out, preferred_element_type=F32) + b_out


CHUNK = 80


def turned(v, shift):
    return pltpu.roll(v, shift % 8, axis=0) if shift % 8 else v


def pack_rows(lines, base):
    place = lax.broadcasted_iota(jnp.int32, lines[0].shape, 0)
    blocks = []
    for k in range(3):
        block = jnp.zeros_like(lines[0])
        for r in range(8):
            low = 3 * r - 8 * k
            if low > -3 and low < 8:
                inside = jnp.logical_and(place >= low, place < low + 3)
                block = jnp.where(inside, turned(lines[r], low - base), block)
        blocks.append(block)
    return blocks


def unpack_row(blocks, r, base):
    first, last = 3 * r // 8, (3 * r + 2) // 8
    value = turned(blocks[first], base - 3 * r + 8 * first)
    if last != first:
        place = lax.broadcasted_iota(jnp.int32, value.shape, 0)
        other = turned(blocks[last], base - 3 * r + 8 * last)
        value = jnp.where(place >= base + 8 * last - 3 * r, other, value)
    return value


def section_kernel(step_rows, tiles_ref, coarse_hbm, dw_hbm, dwb_ref, gain_ref, shift_ref, win_hbm, bin_ref, wout_hbm,
                   bout_ref, scale_ref, y_ref, coarse_ref, dw_ref, win_ref, wout_ref, load_sems, x_ref, wb_ref, d_ref, u_ref, out_ref, edge_out, edge_in,
                   row_out, row_in, corner_in, halo_send, halo_recv, sems, group_sems):
    height, width, channels = coarse_ref.shape
    groups = channels // 128
    lat, lon = lax.axis_index("lat"), lax.axis_index("lon")
    nlat, nlon = lax.axis_size("lat"), lax.axis_size("lon")
    left, right = lax.rem(lon + nlon - 1, nlon), lax.rem(lon + 1, nlon)
    has_up, has_down = lat > 0, lat < nlat - 1
    owned = height // nlon

    loads = [pltpu.make_async_copy(a, b, load_sems.at[n]) for n, (a, b) in enumerate((
        (coarse_hbm, coarse_ref), (dw_hbm, dw_ref), (win_hbm, win_ref), (wout_hbm, wout_ref)))]
    for load in loads:
        load.start()

    barrier = pltpu.get_barrier_semaphore()

    def greet(a, b):
        pl.semaphore_signal(barrier, inc=1, device_id=(a, b), device_id_type=MESH)

    @pl.loop(1, nlon)
    def _(k):
        greet(lat, lax.rem(lon + k, nlon))

    for present, other in ((has_up, lat - 1), (has_down, lat + 1)):
        @pl.when(present)
        def _():
            for b in (left, lon, right):
                greet(other, b)

    @pl.when(jnp.logical_and(has_down, lon == nlon - 1))
    def _():
        @pl.loop(0, nlon)
        def _(k):
            greet(lat + 1, k)

    def edge_copies(l, chunk, count):
        part = pl.ds(pl.multiple_of(chunk * CHUNK, CHUNK), count * CHUNK)
        return [pltpu.make_async_remote_copy(
            src_ref=edge_out.at[l, k, part], dst_ref=edge_in.at[l, k, part],
            send_sem=halo_send.at[l, k], recv_sem=halo_recv.at[l, k],
            device_id=(lat, (left, right)[k]), device_id_type=MESH) for k in range(2)]

    def pack_edges(source, l, i):
        low, high = [], []
        for t in range(3):
            part = pl.ds(pl.multiple_of(t * TS + i * 8, 8), 8)
            begin = source[part, 0:16, :].astype(F32)
            end = source[part, width - 16 : width, :].astype(F32)
            low += pack_rows([begin[r, 0:8] for r in range(8)], 0)
            high += pack_rows([end[r, 8:16] for r in range(8)], 5)
        for k, blocks in enumerate((low, high)):
            blocks = blocks + [jnp.zeros_like(blocks[0])]
            edge_out[l, k, pl.ds(pl.multiple_of(i * CHUNK, CHUNK), CHUNK)] = jnp.concatenate(blocks, 0).astype(BF16)

    def row_copies(l, k):
        other = lat - 1 if k == 0 else lat + 1
        part = pl.ds(0, 32) if k == 0 else pl.ds(4 * CHUNK - 32, 32)
        copies = [pltpu.make_async_remote_copy(
            src_ref=row_out.at[l, k], dst_ref=row_in.at[l, k],
            send_sem=halo_send.at[l, 2 + k], recv_sem=halo_recv.at[l, 2 + k],
            device_id=(other, lon), device_id_type=MESH)]
        for e in range(2):
            copies.append(pltpu.make_async_remote_copy(
                src_ref=edge_out.at[l, e, part], dst_ref=corner_in.at[l, k, e],
                send_sem=halo_send.at[l, 4 + 2 * k + e], recv_sem=halo_recv.at[l, 4 + 2 * k + e],
                device_id=(other, (left, right)[e]), device_id_type=MESH))
        return copies

    m0, m1, m2 = tiles_ref[0, 0], tiles_ref[0, 1], tiles_ref[0, 2]
    first_tile = jnp.where(m0 != 0, 0, 1)
    second_tile = jnp.where(m2 != 0, 2, 1)
    masks = [m.astype(F32) for m in (m0, m1, m2)]

    loads[0].wait()

    @pl.loop(0, 4)
    def _(i):
        pack_edges(coarse_ref, 0, i)

    row_out[0, 0] = coarse_ref[0:3]
    row_out[0, 1] = coarse_ref[height - 3 : height]

    pl.semaphore_wait(barrier, nlon - 1 + jnp.where(has_up, 4, 0) + jnp.where(has_down, 3, 0))
    for k, present in enumerate((has_up, has_down)):
        @pl.when(present)
        def _():
            for copy in row_copies(0, k):
                copy.start()
    for copy in edge_copies(0, 0, 4):
        copy.start()

    @pl.loop(0, height // 8)
    def _(i):
        part = pl.ds(pl.multiple_of(i * 8, 8), 8)
        for g in range(groups):
            x_ref[0, g, pl.ds(i * 8 + 3, 8), COL0 : COL0 + width, :] = coarse_ref[
                part, :, 128 * g : 128 * g + 128].astype(F32)

    def chunk_copy(row, slot, a, b, which):
        return pltpu.make_async_remote_copy(
            src_ref=out_ref.at[row], dst_ref=y_ref.at[slot, pl.ds(pl.multiple_of(lon * width, 32), width)],
            send_sem=group_sems.at[0, which], recv_sem=group_sems.at[1, which],
            device_id=(a, b), device_id_type=MESH)

    def own_copy(row, slot):
        return pltpu.make_async_copy(
            out_ref.at[row], y_ref.at[slot, pl.ds(pl.multiple_of(lon * width, 32), width)], sems.at[slot])

    def send_row(row):
        owner = row // owned
        slot = row - owner * owned

        @pl.when(owner == lon)
        def _():
            own_copy(row, slot).start()

        @pl.when(owner != lon)
        def _():
            chunk_copy(row, slot, lat, owner, 0).start()

        @pl.when(slot == 0)
        def _():
            @pl.when(row == 0)
            def _():
                @pl.when(has_up)
                def _():
                    chunk_copy(row, owned, lat - 1, nlon - 1, 1).start()

            @pl.when(row > 0)
            def _():
                @pl.when(owner - 1 == lon)
                def _():
                    own_copy(row, owned).start()

                @pl.when(owner - 1 != lon)
                def _():
                    chunk_copy(row, owned, lat, owner - 1, 1).start()

    for load in loads[1:]:
        load.wait()

    for l in range(2):
        x = x_ref.at[l]
        rows = step_rows[l]
        blocks = TS // rows
        one = slice(l, l + 1)
        for k in range(49):
            for g in range(groups):
                wb_ref[k, g] = jnp.broadcast_to(dw_ref[k // 7, k % 7, l : l + 1, 128 * g : 128 * g + 128], (8, 128))

        def place_edges():
            for copy in edge_copies(l, 0, 4):
                copy.wait()

            @pl.loop(0, 4)
            def _(i):
                part = pl.ds(pl.multiple_of(i * CHUNK, CHUNK), CHUNK)
                after = edge_in[l, 0, part].astype(F32)
                before = edge_in[l, 1, part].astype(F32)
                for t in range(3):
                    after_blocks = [after[8 * n : 8 * n + 8] for n in range(3 * t, 3 * t + 3)]
                    before_blocks = [before[8 * n : 8 * n + 8] for n in range(3 * t, 3 * t + 3)]
                    for r in range(8):
                        line = 3 + t * TS + i * 8 + r
                        right_part = unpack_row(after_blocks, r, 0)
                        left_part = unpack_row(before_blocks, r, 5)
                        for g in range(groups):
                            lanes = slice(128 * g, 128 * g + 128)
                            x[g, line, COL0 + width : COL0 + width + 8, :] = right_part[:, lanes]
                            x[g, line, 0:8, :] = left_part[:, lanes]

        def place_rows():
            for k, present in enumerate((has_up, has_down)):
                receives = (has_down, has_up)[k]
                place = height + 3 if k == 0 else 0

                @pl.when(present)
                def _():
                    for copy in row_copies(l, k):
                        copy.wait_send()

                @pl.when(receives)
                def _():
                    for copy in row_copies(l, k):
                        copy.wait_recv()
                    middle = row_in[l, k].astype(F32)
                    after = corner_in[l, k, 0].astype(F32)
                    before = corner_in[l, k, 1].astype(F32)
                    after = [after[8 * n : 8 * n + 8] for n in range(3)]
                    before = [before[8 * n : 8 * n + 8] for n in range(3)]
                    for g in range(groups):
                        lanes = slice(128 * g, 128 * g + 128)
                        x[g, place : place + 3, COL0 : COL0 + width, :] = middle[:, :, lanes]
                        for r in range(3):
                            n = r if k == 0 else r + 5
                            x[g, place + r, COL0 + width : COL0 + width + 8, :] = unpack_row(after, n, 0)[:, lanes]
                            x[g, place + r, 0:8, :] = unpack_row(before, n, 5)[:, lanes]

                @pl.when(jnp.logical_not(receives))
                def _():
                    for g in range(groups):
                        x[g, place : place + 3] = jnp.zeros((3, width + 16, 128), F32)

        def depthwise(i, parts):
            @pl.loop(0, 2)
            def _(s):
                tile = jnp.where(s == 0, first_tile, second_tile)
                depthwise_block(x, wb_ref, dwb_ref, l, d_ref.at[s, :, pl.ds(pl.multiple_of(i * rows, rows), rows)],
                                tile * TS + i * rows, rows, groups, parts)

        early = 3

        def block_of(step):
            if l == 0:
                return jnp.where(step < 2, step * (blocks - 1), step - 1)
            return lax.rem(step + lon // 8 * 2 + 4 * lax.rem(lat, 2), blocks)

        if l == 1:
            place_rows()

            @pl.loop(0, early)
            def _(step):
                depthwise(block_of(step), (1, 2))

            place_edges()

        if l == 0:
            @pl.loop(1, blocks - 1)
            def _(i):
                depthwise(i, (1, 2))

            place_rows()

            @pl.loop(0, 2)
            def _(n):
                depthwise(n * (blocks - 1), (1, 2))

            place_edges()

        @pl.loop(0, blocks)
        def _(step):
            i = block_of(step)
            if l == 0:
                depthwise(i, (0, 3))
            else:
                @pl.when(step < early)
                def _():
                    depthwise(i, (0, 3))

                @pl.when(step >= early)
                def _():
                    depthwise(i, (0, 1, 2, 3))

            @pl.loop(0, 2)
            def _(s):
                depth = jnp.concatenate([d_ref[s, g, pl.ds(pl.multiple_of(i * rows, rows), rows)].reshape(rows * width, 128) for g in range(groups)], 1)
                u_ref[s, 0:rows] = mix_block(depth, gain_ref[one], shift_ref[one], win_ref[l], bin_ref[one], wout_ref[l],
                                     bout_ref[one]).reshape(rows, width, channels)

            for t in range(3):
                row0 = pl.multiple_of(t * TS + i * rows, rows)
                place = pl.ds(3 + row0, rows)
                for g in range(groups):
                    lanes = slice(128 * g, 128 * g + 128)
                    if t == 1:
                        update = jnp.where(m0 == 0, u_ref[0, 0:rows, :, lanes], u_ref[1, 0:rows, :, lanes])
                    else:
                        update = u_ref[t // 2, 0:rows, :, lanes]
                    field = x[g, place, COL0 : COL0 + width, :]
                    field = (field + (masks[t] * scale_ref[one, lanes]) * update).astype(BF16)
                    out_ref[pl.ds(row0, rows), :, lanes] = field
                    if l == 0:
                        x_ref[1, g, place, COL0 : COL0 + width, :] = field.astype(F32)
            if l == 0:
                pack_edges(out_ref, 1, i)
                for copy in edge_copies(1, i, 1):
                    copy.start()

                @pl.when(step == 1)
                def _():
                    row_out[1, 0] = out_ref[0:3]
                    row_out[1, 1] = out_ref[height - 3 : height]
                    for k, present in enumerate((has_up, has_down)):
                        @pl.when(present)
                        def _():
                            for copy in row_copies(1, k):
                                copy.start()
            else:
                @pl.loop(0, 3 * rows)
                def _(n):
                    t = lax.rem(n + lat, 3)
                    r = lax.rem(n // 3 * 3 + lon // 2, rows)
                    send_row(t * TS + i * rows + r)

    far = (nlon - 1) * width

    def count_wait(which, sem, n):
        copy = pltpu.make_async_copy(y_ref.at[owned, pl.ds(0, n * width)], y_ref.at[owned, pl.ds(0, n * width)],
                                     group_sems.at[which, sem])
        copy.wait()

    for which in range(2):
        pltpu.make_async_copy(y_ref.at[pl.ds(0, owned), pl.ds(0, far)], y_ref.at[pl.ds(0, owned), pl.ds(0, far)],
                              group_sems.at[which, 0]).wait()
    last = lon == nlon - 1
    sent = nlon - 2 + jnp.where(last, 1, 0) + jnp.where(has_up, 1, 0)
    for n in (nlon - 2, nlon - 1, nlon):
        @pl.when(sent == n)
        def _():
            count_wait(0, 1, n)

    @pl.when(jnp.logical_not(last))
    def _():
        count_wait(1, 1, nlon - 1)

    @pl.when(jnp.logical_and(last, has_down))
    def _():
        count_wait(1, 1, nlon)

    for slot in range(owned):
        own_copy(slot, slot).wait()

    @pl.when(jnp.logical_not(last))
    def _():
        own_copy(0, owned).wait()


def section_call(tiles, coarse, dw, dwb, gain, shift, win, b_in, wout, bout, scale, step_rows=(8, 4)):
    height, width, channels = coarse.shape
    groups = channels // 128
    nlon = lax.axis_size("lon")
    owned = height // nlon
    vmem = pl.BlockSpec(memory_space=pltpu.VMEM)
    hbm = pl.BlockSpec(memory_space=pl.ANY)
    dma = pltpu.SemaphoreType.DMA
    rows = max(step_rows)
    return pl.pallas_call(
        functools.partial(section_kernel, step_rows),
        out_shape=jax.ShapeDtypeStruct((owned + 1, nlon * width, channels), BF16),
        in_specs=[pl.BlockSpec(memory_space=pltpu.SMEM), hbm, hbm, vmem, vmem, vmem, hbm, vmem, hbm, vmem, vmem],
        out_specs=pl.BlockSpec(memory_space=pl.ANY),
        scratch_shapes=[
            pltpu.VMEM(coarse.shape, BF16),
            pltpu.VMEM(dw.shape, F32),
            pltpu.VMEM(win.shape, BF16),
            pltpu.VMEM(wout.shape, BF16),
            dma((4,)),
            pltpu.VMEM((2, groups, height + 6, width + 16, 128), F32),
            pltpu.VMEM((49, groups, 8, 128), F32),
            pltpu.VMEM((2, groups, TS, width, 128), F32),
            pltpu.VMEM((2, rows, width, channels), F32),
            pltpu.VMEM((height, width, channels), BF16),
            pltpu.VMEM((2, 2, 4 * CHUNK, channels), BF16),
            pltpu.VMEM((2, 2, 4 * CHUNK, channels), BF16),
            pltpu.VMEM((2, 2, 3, width, channels), BF16),
            pltpu.VMEM((2, 2, 3, width, channels), BF16),
            pltpu.VMEM((2, 2, 2, 32, channels), BF16),
            dma((2, 8)),
            dma((2, 8)),
            dma((owned + 1,)),
            dma((2, 2)),
        ],
        compiler_params=pltpu.CompilerParams(
            collective_id=0, has_side_effects=True, vmem_limit_bytes=60 * 1024 * 1024),
        cost_estimate=pl.CostEstimate(flops=12_000_000_000, bytes_accessed=10_000_000, transcendentals=0),
    )(tiles, coarse, dw, dwb, gain, shift, win, b_in, wout, bout, scale)


UCH = 512


def nt(w, y):
    return lax.dot_general(w, y, (((1,), (1,)), ((), ())), preferred_element_type=F32)


TAPS = (4, 5, 7, 8, 1, 2, 3, 6, 0)


def upsample_kernel(y_ref, next_ref, wt_ref, bias_ref, out_ref):
    last = jnp.logical_and(lax.axis_index("lat") == lax.axis_size("lat") - 1,
                           lax.axis_index("lon") == lax.axis_size("lon") - 1)
    valid = jnp.logical_not(last)

    def weights(begin, end):
        return jnp.concatenate([wt_ref[n] for n in TAPS[begin:end]], 0)

    width_out = out_ref.shape[1]
    row = lax.broadcasted_iota(jnp.int32, (256, 256), 0)
    col = lax.broadcasted_iota(jnp.int32, (256, 256), 1)
    order = jnp.where(row == (col % 2) * 128 + col // 2, 1.0, 0.0).astype(BF16)
    direct, beside = [], []
    for i in range(4):
        cur, after = y_ref[i], next_ref[i]
        if i == 3:
            cur = jnp.where(valid, cur, jnp.zeros_like(cur))
            after = jnp.where(valid, after, jnp.zeros_like(after))
        both = jnp.concatenate([cur, after], 0).astype(F32)
        right = both[1 : 1 + UCH].astype(BF16)
        begin, end = (4 if i == 3 else 0, 4 if i == 0 else 6)
        values = nt(weights(begin, end), cur)
        direct.append({begin + n: values[n * width_out : (n + 1) * width_out] for n in range(end - begin)})
        begin, end = (8 if i == 3 else 6, 8 if i == 0 else 9)
        values = nt(weights(begin, end), right)
        beside.append({begin + n: values[n * width_out : (n + 1) * width_out] for n in range(end - begin)})
    same = lax.broadcasted_iota(jnp.int32, (width_out, width_out), 0) == lax.broadcasted_iota(
        jnp.int32, (width_out, width_out), 1)
    bias = jnp.sum(jnp.where(same, bias_ref[...], 0.0), axis=1, keepdims=True)
    for i in range(3):
        ee = direct[i][0] + bias
        eo = direct[i][1] + beside[i][6] + bias
        oe = direct[i][2] + direct[i + 1][4] + bias
        oo = direct[i][3] + beside[i][7] + direct[i + 1][5] + beside[i + 1][8] + bias
        for p, (even, odd) in enumerate(((ee, eo), (oe, oo))):
            even, odd = even.astype(BF16), odd.astype(BF16)
            for k in range(UCH // 128):
                lanes = slice(128 * k, 128 * k + 128)
                pair = jnp.concatenate([even[:, lanes], odd[:, lanes]], 1)
                out_ref[2 * i + p, :, 256 * k : 256 * k + 256] = jnp.dot(
                    pair, order, preferred_element_type=F32).astype(BF16)


def upsample_call(y, weight, bias):
    rows, width, channels = y.shape
    out_width = weight.shape[3]
    wt = weight.transpose(0, 1, 3, 2).reshape(9, out_width, channels)
    chunks = width // UCH
    bias = bias.reshape(1, -1)
    whole = lambda w: pl.BlockSpec(w.shape, lambda j: (0,) * w.ndim)
    out = pl.pallas_call(
        upsample_kernel,
        grid=(chunks,),
        out_shape=jax.ShapeDtypeStruct((2 * rows - 2, out_width, 2 * width), BF16),
        in_specs=[
            pl.BlockSpec((rows, UCH, channels), lambda j: (0, j, 0)),
            pl.BlockSpec((rows, 16, channels), lambda j: (0, ((j + 1) % chunks) * (UCH // 16), 0)),
            whole(wt), whole(bias),
        ],
        out_specs=pl.BlockSpec((2 * rows - 2, out_width, 2 * UCH), lambda j: (0, 0, j)),
        compiler_params=pltpu.CompilerParams(vmem_limit_bytes=60 * 1024 * 1024),
    )(y, y, wt, bias)
    return out.transpose(0, 2, 1)


def local(coarse, ocean_tiles, dw_weight, dw_bias, norm_gain, norm_shift, in_weight, in_bias,
          out_weight, out_bias, layer_scale, up_weight, up_bias):
    rows = section_call(ocean_tiles.T, coarse, dw_weight.transpose(1, 2, 0, 3), dw_bias, norm_gain, norm_shift,
                        in_weight, in_bias, out_weight, out_bias, layer_scale)
    return upsample_call(rows, up_weight, up_bias)


def solution(mesh):
    placed = (P("lat", "lon", None), P("lat", "lon")) + (P(),) * 11
    return jax.shard_map(
        local, mesh=mesh, in_specs=placed, out_specs=P(("lat", "lon"), None, None), check_vma=False
    )
```

```python
import functools
import jax
import jax.numpy as jnp
from jax import lax
from jax.experimental import pallas as pl
from jax.experimental.pallas import tpu as pltpu
from jax.sharding import PartitionSpec as P

TS = 32
COL0 = 8
MESH = pl.DeviceIdType.MESH
F32 = jnp.float32
BF16 = jnp.bfloat16


def depthwise_block(x_ref, wb_ref, bias_ref, l, d_ref, row0, rows, groups, parts):
    for g in range(groups):
        for cb in parts:
            total = jnp.zeros((rows, 8, 128), F32)
            for b in range(7):
                start = COL0 - 3 + b + 8 * cb
                window = x_ref[g, pl.ds(row0, rows + 6), start : start + 8, :]
                for a in range(7):
                    total = total + window[a : a + rows] * wb_ref[a * 7 + b, g]
            d_ref[g, :, 8 * cb : 8 * cb + 8, :] = total + bias_ref[l : l + 1, 128 * g : 128 * g + 128]


def mix_block(depth, gain, shift, w_in, b_in, w_out, b_out):
    center = jnp.mean(depth, -1, keepdims=True)
    offset = depth - center
    spread = jnp.mean(offset * offset, -1, keepdims=True)
    normed = (offset * lax.rsqrt(spread + 1e-06) * gain + shift).astype(BF16)
    hidden = jnp.dot(normed, w_in, preferred_element_type=F32) + b_in
    inner = hidden * (0.7978845608028654 + 0.035677408136300125 * (hidden * hidden))
    half = 0.5 * hidden
    hidden = (half + half * jnp.tanh(inner)).astype(BF16)
    return jnp.dot(hidden, w_out, preferred_element_type=F32) + b_out


CHUNK = 80


def turned(v, shift):
    return pltpu.roll(v, shift % 8, axis=0) if shift % 8 else v


def pack_rows(lines, base):
    place = lax.broadcasted_iota(jnp.int32, lines[0].shape, 0)
    blocks = []
    for k in range(3):
        block = jnp.zeros_like(lines[0])
        for r in range(8):
            low = 3 * r - 8 * k
            if low > -3 and low < 8:
                inside = jnp.logical_and(place >= low, place < low + 3)
                block = jnp.where(inside, turned(lines[r], low - base), block)
        blocks.append(block)
    return blocks


def unpack_row(blocks, r, base):
    first, last = 3 * r // 8, (3 * r + 2) // 8
    value = turned(blocks[first], base - 3 * r + 8 * first)
    if last != first:
        place = lax.broadcasted_iota(jnp.int32, value.shape, 0)
        other = turned(blocks[last], base - 3 * r + 8 * last)
        value = jnp.where(place >= base + 8 * last - 3 * r, other, value)
    return value


def section_kernel(step_rows, tiles_ref, coarse_hbm, dw_hbm, dwb_ref, gain_ref, shift_ref, win_hbm, bin_ref, wout_hbm,
                   bout_ref, scale_ref, y_ref, coarse_ref, dw_ref, win_ref, wout_ref, load_sems, x_ref, wb_ref, d_ref, u_ref, out_ref, edge_out, edge_in,
                   row_out, row_in, corner_in, halo_send, halo_recv, sems, group_sems):
    height, width, channels = coarse_ref.shape
    groups = channels // 128
    lat, lon = lax.axis_index("lat"), lax.axis_index("lon")
    nlat, nlon = lax.axis_size("lat"), lax.axis_size("lon")
    left, right = lax.rem(lon + nlon - 1, nlon), lax.rem(lon + 1, nlon)
    has_up, has_down = lat > 0, lat < nlat - 1
    owned = height // nlon

    loads = [pltpu.make_async_copy(a, b, load_sems.at[n]) for n, (a, b) in enumerate((
        (coarse_hbm, coarse_ref), (dw_hbm, dw_ref), (win_hbm, win_ref), (wout_hbm, wout_ref)))]
    for load in loads:
        load.start()

    barrier = pltpu.get_barrier_semaphore()

    def greet(a, b):
        pl.semaphore_signal(barrier, inc=1, device_id=(a, b), device_id_type=MESH)

    @pl.loop(1, nlon)
    def _(k):
        greet(lat, lax.rem(lon + k, nlon))

    for present, other in ((has_up, lat - 1), (has_down, lat + 1)):
        @pl.when(present)
        def _():
            for b in (left, lon, right):
                greet(other, b)

    @pl.when(jnp.logical_and(has_down, lon == nlon - 1))
    def _():
        @pl.loop(0, nlon)
        def _(k):
            greet(lat + 1, k)

    def edge_copies(l, chunk, count):
        part = pl.ds(pl.multiple_of(chunk * CHUNK, CHUNK), count * CHUNK)
        return [pltpu.make_async_remote_copy(
            src_ref=edge_out.at[l, k, part], dst_ref=edge_in.at[l, k, part],
            send_sem=halo_send.at[l, k], recv_sem=halo_recv.at[l, k],
            device_id=(lat, (left, right)[k]), device_id_type=MESH) for k in range(2)]

    def pack_edges(source, l, i):
        low, high = [], []
        for t in range(3):
            part = pl.ds(pl.multiple_of(t * TS + i * 8, 8), 8)
            begin = source[part, 0:16, :].astype(F32)
            end = source[part, width - 16 : width, :].astype(F32)
            low += pack_rows([begin[r, 0:8] for r in range(8)], 0)
            high += pack_rows([end[r, 8:16] for r in range(8)], 5)
        for k, blocks in enumerate((low, high)):
            blocks = blocks + [jnp.zeros_like(blocks[0])]
            edge_out[l, k, pl.ds(pl.multiple_of(i * CHUNK, CHUNK), CHUNK)] = jnp.concatenate(blocks, 0).astype(BF16)

    def row_copies(l, k):
        other = lat - 1 if k == 0 else lat + 1
        part = pl.ds(0, 32) if k == 0 else pl.ds(4 * CHUNK - 32, 32)
        copies = [pltpu.make_async_remote_copy(
            src_ref=row_out.at[l, k], dst_ref=row_in.at[l, k],
            send_sem=halo_send.at[l, 2 + k], recv_sem=halo_recv.at[l, 2 + k],
            device_id=(other, lon), device_id_type=MESH)]
        for e in range(2):
            copies.append(pltpu.make_async_remote_copy(
                src_ref=edge_out.at[l, e, part], dst_ref=corner_in.at[l, k, e],
                send_sem=halo_send.at[l, 4 + 2 * k + e], recv_sem=halo_recv.at[l, 4 + 2 * k + e],
                device_id=(other, (left, right)[e]), device_id_type=MESH))
        return copies

    m0, m1, m2 = tiles_ref[0, 0], tiles_ref[0, 1], tiles_ref[0, 2]
    first_tile = jnp.where(m0 != 0, 0, 1)
    second_tile = jnp.where(m2 != 0, 2, 1)
    masks = [m.astype(F32) for m in (m0, m1, m2)]

    loads[0].wait()

    @pl.loop(0, 4)
    def _(i):
        pack_edges(coarse_ref, 0, i)

    row_out[0, 0] = coarse_ref[0:3]
    row_out[0, 1] = coarse_ref[height - 3 : height]

    pl.semaphore_wait(barrier, nlon - 1 + jnp.where(has_up, 4, 0) + jnp.where(has_down, 3, 0))
    for k, present in enumerate((has_up, has_down)):
        @pl.when(present)
        def _():
            for copy in row_copies(0, k):
                copy.start()
    for copy in edge_copies(0, 0, 4):
        copy.start()

    @pl.loop(0, height // 8)
    def _(i):
        part = pl.ds(pl.multiple_of(i * 8, 8), 8)
        for g in range(groups):
            x_ref[0, g, pl.ds(i * 8 + 3, 8), COL0 : COL0 + width, :] = coarse_ref[
                part, :, 128 * g : 128 * g + 128].astype(F32)

    def chunk_copy(row, slot, a, b, which):
        return pltpu.make_async_remote_copy(
            src_ref=out_ref.at[row], dst_ref=y_ref.at[slot, pl.ds(pl.multiple_of(lon * width, 32), width)],
            send_sem=group_sems.at[0, which], recv_sem=group_sems.at[1, which],
            device_id=(a, b), device_id_type=MESH)

    def own_copy(row, slot):
        return pltpu.make_async_copy(
            out_ref.at[row], y_ref.at[slot, pl.ds(pl.multiple_of(lon * width, 32), width)], sems.at[slot])

    def send_row(row):
        owner = row // owned
        slot = row - owner * owned

        @pl.when(owner == lon)
        def _():
            own_copy(row, slot).start()

        @pl.when(owner != lon)
        def _():
            chunk_copy(row, slot, lat, owner, 0).start()

        @pl.when(slot == 0)
        def _():
            @pl.when(row == 0)
            def _():
                @pl.when(has_up)
                def _():
                    chunk_copy(row, owned, lat - 1, nlon - 1, 1).start()

            @pl.when(row > 0)
            def _():
                @pl.when(owner - 1 == lon)
                def _():
                    own_copy(row, owned).start()

                @pl.when(owner - 1 != lon)
                def _():
                    chunk_copy(row, owned, lat, owner - 1, 1).start()

    for load in loads[1:]:
        load.wait()

    for l in range(2):
        x = x_ref.at[l]
        rows = step_rows[l]
        blocks = TS // rows
        one = slice(l, l + 1)
        for k in range(49):
            for g in range(groups):
                wb_ref[k, g] = jnp.broadcast_to(dw_ref[k // 7, k % 7, l : l + 1, 128 * g : 128 * g + 128], (8, 128))

        def place_edges():
            for copy in edge_copies(l, 0, 4):
                copy.wait()

            @pl.loop(0, 4)
            def _(i):
                part = pl.ds(pl.multiple_of(i * CHUNK, CHUNK), CHUNK)
                after = edge_in[l, 0, part].astype(F32)
                before = edge_in[l, 1, part].astype(F32)
                for t in range(3):
                    after_blocks = [after[8 * n : 8 * n + 8] for n in range(3 * t, 3 * t + 3)]
                    before_blocks = [before[8 * n : 8 * n + 8] for n in range(3 * t, 3 * t + 3)]
                    for r in range(8):
                        line = 3 + t * TS + i * 8 + r
                        right_part = unpack_row(after_blocks, r, 0)
                        left_part = unpack_row(before_blocks, r, 5)
                        for g in range(groups):
                            lanes = slice(128 * g, 128 * g + 128)
                            x[g, line, COL0 + width : COL0 + width + 8, :] = right_part[:, lanes]
                            x[g, line, 0:8, :] = left_part[:, lanes]

        def place_rows():
            for k, present in enumerate((has_up, has_down)):
                receives = (has_down, has_up)[k]
                place = height + 3 if k == 0 else 0

                @pl.when(present)
                def _():
                    for copy in row_copies(l, k):
                        copy.wait_send()

                @pl.when(receives)
                def _():
                    for copy in row_copies(l, k):
                        copy.wait_recv()
                    middle = row_in[l, k].astype(F32)
                    after = corner_in[l, k, 0].astype(F32)
                    before = corner_in[l, k, 1].astype(F32)
                    after = [after[8 * n : 8 * n + 8] for n in range(3)]
                    before = [before[8 * n : 8 * n + 8] for n in range(3)]
                    for g in range(groups):
                        lanes = slice(128 * g, 128 * g + 128)
                        x[g, place : place + 3, COL0 : COL0 + width, :] = middle[:, :, lanes]
                        for r in range(3):
                            n = r if k == 0 else r + 5
                            x[g, place + r, COL0 + width : COL0 + width + 8, :] = unpack_row(after, n, 0)[:, lanes]
                            x[g, place + r, 0:8, :] = unpack_row(before, n, 5)[:, lanes]

                @pl.when(jnp.logical_not(receives))
                def _():
                    for g in range(groups):
                        x[g, place : place + 3] = jnp.zeros((3, width + 16, 128), F32)

        def depthwise(i, parts):
            @pl.loop(0, 2)
            def _(s):
                tile = jnp.where(s == 0, first_tile, second_tile)
                depthwise_block(x, wb_ref, dwb_ref, l, d_ref.at[s, :, pl.ds(pl.multiple_of(i * rows, rows), rows)],
                                tile * TS + i * rows, rows, groups, parts)

        early = 5

        def block_of(step):
            if l == 0:
                return jnp.where(step < 2, step * (blocks - 1), step - 1)
            return lax.rem(step + lon // 8 * 2 + 4 * lax.rem(lat, 2), blocks)

        if l == 1:
            place_rows()

            @pl.loop(0, early)
            def _(step):
                depthwise(block_of(step), (1, 2))

            place_edges()

        if l == 0:
            @pl.loop(1, blocks - 1)
            def _(i):
                depthwise(i, (1, 2))

            place_rows()

            @pl.loop(0, 2)
            def _(n):
                depthwise(n * (blocks - 1), (1, 2))

            place_edges()

        @pl.loop(0, blocks)
        def _(step):
            i = block_of(step)
            if l == 0:
                depthwise(i, (0, 3))
            else:
                @pl.when(step < early)
                def _():
                    depthwise(i, (0, 3))

                @pl.when(step >= early)
                def _():
                    depthwise(i, (0, 1, 2, 3))

            @pl.loop(0, 2)
            def _(s):
                depth = jnp.concatenate([d_ref[s, g, pl.ds(pl.multiple_of(i * rows, rows), rows)].reshape(rows * width, 128) for g in range(groups)], 1)
                u_ref[s, 0:rows] = mix_block(depth, gain_ref[one], shift_ref[one], win_ref[l], bin_ref[one], wout_ref[l],
                                     bout_ref[one]).reshape(rows, width, channels)

            for t in range(3):
                row0 = pl.multiple_of(t * TS + i * rows, rows)
                place = pl.ds(3 + row0, rows)
                for g in range(groups):
                    lanes = slice(128 * g, 128 * g + 128)
                    if t == 1:
                        update = jnp.where(m0 == 0, u_ref[0, 0:rows, :, lanes], u_ref[1, 0:rows, :, lanes])
                    else:
                        update = u_ref[t // 2, 0:rows, :, lanes]
                    field = x[g, place, COL0 : COL0 + width, :]
                    field = (field + (masks[t] * scale_ref[one, lanes]) * update).astype(BF16)
                    out_ref[pl.ds(row0, rows), :, lanes] = field
                    if l == 0:
                        x_ref[1, g, place, COL0 : COL0 + width, :] = field.astype(F32)
            if l == 0:
                pack_edges(out_ref, 1, i)
                for copy in edge_copies(1, i, 1):
                    copy.start()

                @pl.when(step == 1)
                def _():
                    row_out[1, 0] = out_ref[0:3]
                    row_out[1, 1] = out_ref[height - 3 : height]
                    for k, present in enumerate((has_up, has_down)):
                        @pl.when(present)
                        def _():
                            for copy in row_copies(1, k):
                                copy.start()
            else:
                @pl.loop(0, 3 * rows)
                def _(n):
                    t = lax.rem(n + lat, 3)
                    r = lax.rem(n // 3 * 3 + lon // 2, rows)
                    send_row(t * TS + i * rows + r)

    far = (nlon - 1) * width

    def count_wait(which, sem, n):
        copy = pltpu.make_async_copy(y_ref.at[owned, pl.ds(0, n * width)], y_ref.at[owned, pl.ds(0, n * width)],
                                     group_sems.at[which, sem])
        copy.wait()

    for which in range(2):
        pltpu.make_async_copy(y_ref.at[pl.ds(0, owned), pl.ds(0, far)], y_ref.at[pl.ds(0, owned), pl.ds(0, far)],
                              group_sems.at[which, 0]).wait()
    last = lon == nlon - 1
    sent = nlon - 2 + jnp.where(last, 1, 0) + jnp.where(has_up, 1, 0)
    for n in (nlon - 2, nlon - 1, nlon):
        @pl.when(sent == n)
        def _():
            count_wait(0, 1, n)

    @pl.when(jnp.logical_not(last))
    def _():
        count_wait(1, 1, nlon - 1)

    @pl.when(jnp.logical_and(last, has_down))
    def _():
        count_wait(1, 1, nlon)

    for slot in range(owned):
        own_copy(slot, slot).wait()

    @pl.when(jnp.logical_not(last))
    def _():
        own_copy(0, owned).wait()


def section_call(tiles, coarse, dw, dwb, gain, shift, win, b_in, wout, bout, scale, step_rows=(8, 4)):
    height, width, channels = coarse.shape
    groups = channels // 128
    nlon = lax.axis_size("lon")
    owned = height // nlon
    vmem = pl.BlockSpec(memory_space=pltpu.VMEM)
    hbm = pl.BlockSpec(memory_space=pl.ANY)
    dma = pltpu.SemaphoreType.DMA
    rows = max(step_rows)
    return pl.pallas_call(
        functools.partial(section_kernel, step_rows),
        out_shape=jax.ShapeDtypeStruct((owned + 1, nlon * width, channels), BF16),
        in_specs=[pl.BlockSpec(memory_space=pltpu.SMEM), hbm, hbm, vmem, vmem, vmem, hbm, vmem, hbm, vmem, vmem],
        out_specs=pl.BlockSpec(memory_space=pl.ANY),
        scratch_shapes=[
            pltpu.VMEM(coarse.shape, BF16),
            pltpu.VMEM(dw.shape, F32),
            pltpu.VMEM(win.shape, BF16),
            pltpu.VMEM(wout.shape, BF16),
            dma((4,)),
            pltpu.VMEM((2, groups, height + 6, width + 16, 128), F32),
            pltpu.VMEM((49, groups, 8, 128), F32),
            pltpu.VMEM((2, groups, TS, width, 128), F32),
            pltpu.VMEM((2, rows, width, channels), F32),
            pltpu.VMEM((height, width, channels), BF16),
            pltpu.VMEM((2, 2, 4 * CHUNK, channels), BF16),
            pltpu.VMEM((2, 2, 4 * CHUNK, channels), BF16),
            pltpu.VMEM((2, 2, 3, width, channels), BF16),
            pltpu.VMEM((2, 2, 3, width, channels), BF16),
            pltpu.VMEM((2, 2, 2, 32, channels), BF16),
            dma((2, 8)),
            dma((2, 8)),
            dma((owned + 1,)),
            dma((2, 2)),
        ],
        compiler_params=pltpu.CompilerParams(
            collective_id=0, has_side_effects=True, vmem_limit_bytes=60 * 1024 * 1024),
        cost_estimate=pl.CostEstimate(flops=12_000_000_000, bytes_accessed=10_000_000, transcendentals=0),
    )(tiles, coarse, dw, dwb, gain, shift, win, b_in, wout, bout, scale)


UCH = 512


def nt(w, y):
    return lax.dot_general(w, y, (((1,), (1,)), ((), ())), preferred_element_type=F32)


TAPS = (4, 5, 7, 8, 1, 2, 3, 6, 0)


def upsample_kernel(y_ref, next_ref, wt_ref, bias_ref, out_ref):
    last = jnp.logical_and(lax.axis_index("lat") == lax.axis_size("lat") - 1,
                           lax.axis_index("lon") == lax.axis_size("lon") - 1)
    valid = jnp.logical_not(last)

    def weights(begin, end):
        return jnp.concatenate([wt_ref[n] for n in TAPS[begin:end]], 0)

    width_out = out_ref.shape[1]
    row = lax.broadcasted_iota(jnp.int32, (256, 256), 0)
    col = lax.broadcasted_iota(jnp.int32, (256, 256), 1)
    order = jnp.where(row == (col % 2) * 128 + col // 2, 1.0, 0.0).astype(BF16)
    direct, beside = [], []
    for i in range(4):
        cur, after = y_ref[i], next_ref[i]
        if i == 3:
            cur = jnp.where(valid, cur, jnp.zeros_like(cur))
            after = jnp.where(valid, after, jnp.zeros_like(after))
        both = jnp.concatenate([cur, after], 0).astype(F32)
        right = both[1 : 1 + UCH].astype(BF16)
        begin, end = (4 if i == 3 else 0, 4 if i == 0 else 6)
        values = nt(weights(begin, end), cur)
        direct.append({begin + n: values[n * width_out : (n + 1) * width_out] for n in range(end - begin)})
        begin, end = (8 if i == 3 else 6, 8 if i == 0 else 9)
        values = nt(weights(begin, end), right)
        beside.append({begin + n: values[n * width_out : (n + 1) * width_out] for n in range(end - begin)})
    same = lax.broadcasted_iota(jnp.int32, (width_out, width_out), 0) == lax.broadcasted_iota(
        jnp.int32, (width_out, width_out), 1)
    bias = jnp.sum(jnp.where(same, bias_ref[...], 0.0), axis=1, keepdims=True)
    for i in range(3):
        ee = direct[i][0] + bias
        eo = direct[i][1] + beside[i][6] + bias
        oe = direct[i][2] + direct[i + 1][4] + bias
        oo = direct[i][3] + beside[i][7] + direct[i + 1][5] + beside[i + 1][8] + bias
        for p, (even, odd) in enumerate(((ee, eo), (oe, oo))):
            even, odd = even.astype(BF16), odd.astype(BF16)
            for k in range(UCH // 128):
                lanes = slice(128 * k, 128 * k + 128)
                pair = jnp.concatenate([even[:, lanes], odd[:, lanes]], 1)
                out_ref[2 * i + p, :, 256 * k : 256 * k + 256] = jnp.dot(
                    pair, order, preferred_element_type=F32).astype(BF16)


def upsample_call(y, weight, bias):
    rows, width, channels = y.shape
    out_width = weight.shape[3]
    wt = weight.transpose(0, 1, 3, 2).reshape(9, out_width, channels)
    chunks = width // UCH
    bias = bias.reshape(1, -1)
    whole = lambda w: pl.BlockSpec(w.shape, lambda j: (0,) * w.ndim)
    out = pl.pallas_call(
        upsample_kernel,
        grid=(chunks,),
        out_shape=jax.ShapeDtypeStruct((2 * rows - 2, out_width, 2 * width), BF16),
        in_specs=[
            pl.BlockSpec((rows, UCH, channels), lambda j: (0, j, 0)),
            pl.BlockSpec((rows, 16, channels), lambda j: (0, ((j + 1) % chunks) * (UCH // 16), 0)),
            whole(wt), whole(bias),
        ],
        out_specs=pl.BlockSpec((2 * rows - 2, out_width, 2 * UCH), lambda j: (0, 0, j)),
        compiler_params=pltpu.CompilerParams(vmem_limit_bytes=60 * 1024 * 1024),
    )(y, y, wt, bias)
    return out.transpose(0, 2, 1)


def local(coarse, ocean_tiles, dw_weight, dw_bias, norm_gain, norm_shift, in_weight, in_bias,
          out_weight, out_bias, layer_scale, up_weight, up_bias):
    rows = section_call(ocean_tiles.T, coarse, dw_weight.transpose(1, 2, 0, 3), dw_bias, norm_gain, norm_shift,
                        in_weight, in_bias, out_weight, out_bias, layer_scale)
    return upsample_call(rows, up_weight, up_bias)


def solution(mesh):
    placed = (P("lat", "lon", None), P("lat", "lon")) + (P(),) * 11
    return jax.shard_map(
        local, mesh=mesh, in_specs=placed, out_specs=P(("lat", "lon"), None, None), check_vma=False
    )
```
